128 devices in a mesh: seq: 4 (over x), rows: 8 (over z, core), expert: 4 (over y).
Axes of the slice: x: 4, y: 4, z: 4, core: 2. Of those that a mesh axis runs over, the one named last changes fastest.
Arguments:
- queries: bfloat16 [64, 6144], P(('rows', 'expert')), may hold values from -8 to 8
- k_cache: bfloat16 [64, 3072, 1024], P(('rows', 'expert'), 'seq'), may hold values from -12 to 12
- v_cache: bfloat16 [64, 3072, 1024], P(('rows', 'expert'), 'seq'), may hold values from -6 to 6
- k_new: bfloat16 [64, 1024], P(('rows', 'expert')), may hold values from -10 to 10
- v_new: bfloat16 [64, 1024], P(('rows', 'expert')), may hold values from -6 to 6
- lengths: int32 [64], P(('rows', 'expert')), may hold values from 2 to 3072, as said below
- residual: bfloat16 [64, 6144], P(('rows', 'expert')), may hold values from -60 to 60
- norm_gain: float32 [6144], replicated, may hold values from 0.1 to 1.9
- expert_ids: int32 [64, 2], P(('rows', 'expert')), may hold values from 0 to 3, all different within a row; in each aligned block of 2 rows (0 to 1, 2 to 3, ...) at most 2 rows name the same one
- combine_weights: float32 [64, 2], P(('rows', 'expert')), may hold values from 0.2 to 1
- w_gate: bfloat16 [4, 6144, 16384], P('expert', None, ('seq', 'rows')), may hold values from -0.078125 to 0.078125
- w_up: bfloat16 [4, 6144, 16384], P('expert', None, ('seq', 'rows')), may hold values from -0.078125 to 0.078125
- w_down: bfloat16 [4, 16384, 6144], P('expert', ('seq', 'rows')), may hold values from -0.046875 to 0.046875
Outputs:
- hidden_state: bfloat16 [64, 6144], P(('rows', 'expert'), 'seq')
- layer_out: bfloat16 [64, 6144], P(('rows', 'expert'), 'seq')
The draws below stay inside these ranges and needn't reach their ends.
Inputs may be any that keep to these rules, and one draw needn't show every extreme that they name: `lengths`: the new token is not among them. `expert_ids`: each row names two different experts; within the rows of one group of seq devices (aligned blocks of 2 rows) an expert is named by at most 2 rows.
All inputs are finite; a program needn't handle non-finite values.
Results may differ from the reference program's by a relative error of at most 0.011.
Values may be sent and summed in bfloat16 or wider, within the bound.
No kernel may reach another device: no remote copies, remote signals or barrier semaphores. Data moves between devices by JAX's collectives and lax.ppermute only.
A program may use at most 128 MiB of HBM per device.

```python
import math
import jax
import jax.numpy as jnp
import numpy as np
from jax import lax

D = 6144
HEADS = 48
KV_HEADS = 8
HEAD_DIM = 128
FF = 16384
ROW_DEV = 2
EXPERTS = 4
ROWS = 64
CTX = 3072


def common_draw(key):
    base_key = jax.random.fold_in(key, 101)
    keys = jax.random.split(base_key, 5)
    drawn = jax.random.randint(keys[0], (ROWS,), 2, CTX + 1)
    longest = jax.random.randint(keys[1], (), 0, ROWS)
    lengths = jnp.where(jnp.arange(ROWS) == longest, CTX, drawn)
    first_pos = jax.random.randint(keys[2], (ROWS,), 0, lengths)
    offset = jax.random.randint(keys[3], (ROWS,), 1, lengths)
    second_pos = (first_pos + offset) % lengths
    pattern = jnp.where(jax.random.bernoulli(keys[4], 0.5, (ROWS, KV_HEADS * HEAD_DIM)), 1.0, -1.0)
    return (lengths, first_pos, second_pos, pattern)


def drawn_strength():
    row_index = jnp.arange(ROWS)
    aligned = row_index % 4 == 0
    strength = 5.0 + 1.5 * (row_index // 4 % 3).astype(jnp.float32)
    return (aligned, strength)


def draw_lengths(key, part):
    lengths, first_pos, second_pos, pattern = common_draw(key)
    return lengths.astype(jnp.int32)


def draw_queries(key, part):
    lengths, first_pos, second_pos, pattern = common_draw(key)
    key = jax.random.fold_in(key, 2)
    base = jnp.clip(jax.random.normal(key, (ROWS, D), jnp.float32), -5.0, 5.0)
    aligned, strength = drawn_strength()
    spread = jnp.broadcast_to(pattern.reshape(ROWS, KV_HEADS, 1, HEAD_DIM), (ROWS, KV_HEADS, HEADS // KV_HEADS, HEAD_DIM)).reshape(ROWS, D)
    values = jnp.where(aligned[:, None], strength[:, None] * spread, base)
    return values.astype(jnp.bfloat16)


def draw_k_cache(key, part):
    lengths, first_pos, second_pos, pattern = common_draw(key)
    key = jax.random.fold_in(key, 3)
    base = jnp.clip(2.0 * jax.random.normal(key, (ROWS, CTX, KV_HEADS * HEAD_DIM), jnp.float32), -8.0, 8.0)
    aligned, strength = drawn_strength()
    changed = jnp.maximum(jnp.floor(2.0 * math.sqrt(HEAD_DIM) / strength + 0.5), 1.0)
    coord = (jnp.arange(KV_HEADS * HEAD_DIM) % HEAD_DIM).astype(jnp.float32)
    second_key = jnp.where(coord[None, :] < changed[:, None], 11.0, 12.0) * pattern
    first_key = 12.0 * pattern
    alive = aligned[:, None, None]
    position = jnp.arange(CTX)[None, :, None]
    at_first = position == first_pos[:, None, None]
    at_second = position == second_pos[:, None, None]
    values = jnp.where(alive & at_first, first_key[:, None, :], base)
    values = jnp.where(alive & at_second & jnp.logical_not(at_first), second_key[:, None, :], values)
    return values.astype(jnp.bfloat16)


def draw_residual(key, part):
    key = jax.random.fold_in(key, 4)
    keys = jax.random.split(key, 3)
    base = jnp.clip(jax.random.normal(keys[0], (ROWS, D), jnp.float32), -5.0, 5.0)
    row_scale = jnp.exp(jax.random.uniform(keys[1], (ROWS, 1), jnp.float32, math.log(0.3), math.log(3.0)))
    col_scale = jnp.exp(jax.random.uniform(keys[2], (1, D), jnp.float32, math.log(0.3), math.log(3.0)))
    return (base * row_scale * col_scale).astype(jnp.bfloat16)


def block_levels(stream_key, extent, cuts, smallest, high):
    gain, own = 1.0, jax.random.fold_in(stream_key, 6)
    for dim, shards_of in cuts:
        steps = jnp.exp(jax.random.uniform(jax.random.fold_in(own, dim), (shards_of,), jnp.float32, smallest / len(cuts), high / len(cuts)))
        gain = gain * jnp.repeat(steps, extent[dim] // shards_of).reshape([-1 if axis == dim else 1 for axis in range(len(extent))])
    return gain


def shared_out(stream_key, own, number, rows, count, top, bound, slope):
    order = jax.random.permutation(stream_key, count)
    heavy_load, common = shares(count, rows * top, bound, slope, True), shares(count, rows * top, bound, slope, False)
    places = jnp.arange(count)

    def named(tallies, offset_by):
        used = int((tallies > 0).sum())
        fixed = max(1, used // 4)
        shifted = fixed + (places - fixed + offset_by * (used - fixed)) % max(1, count - fixed)
        return jnp.zeros((count,), jnp.int32).at[order[jnp.where(places < fixed, places, shifted)]].set(jnp.asarray(tallies, jnp.int32))

    tallies = jnp.where(number % 4 == 0, named(heavy_load, number // 4), named(common, number - number // 4 - 1))
    mixed = jax.random.permutation(jax.random.fold_in(own, 3), count)
    donor, taker = mixed[0:count // 2 * 2:2], mixed[1:count // 2 * 2:2]
    margin = jnp.minimum(tallies[donor] - 1, bound - tallies[taker]) // 2
    margin = jnp.where((donor == order[0]) | (taker == order[0]) | (tallies[taker] == 0), 0, jnp.maximum(margin, 0))
    shifted = jax.random.randint(jax.random.fold_in(own, 4), (count // 2,), 0, 1 << 20) % (margin + 1)
    tallies = tallies.at[donor].add(-shifted).at[taker].add(shifted)
    items = jnp.searchsorted(jnp.cumsum(tallies), jnp.arange(rows * top), side="right").astype(jnp.int32)
    grid = items.reshape(top, rows).T
    grid = grid[jax.random.permutation(jax.random.fold_in(own, 1), rows)]
    offset_by = jax.random.randint(jax.random.fold_in(own, 2), (rows, 1), 0, top)
    return jnp.take_along_axis(grid, (jnp.arange(top)[None, :] + offset_by) % top, axis=1)


def shares(amount, total, limit, lean, full):
    portions = [(1 << 20) // math.isqrt(rank ** lean) + 1 for rank in range(1, amount + 1)]
    largest = limit if full else min(limit, max(-(-total // amount), total * portions[0] // sum(portions)))
    least = 1 if total - largest >= amount - 1 else 0
    given, surplus = [largest] + [least] * (amount - 1), total - largest - least * (amount - 1)
    while surplus > 0:
        free = [i for i in range(1, amount) if given[i] < largest] or [i for i in range(1, amount) if given[i] < limit]
        mass, budget = sum([portions[i] for i in free]), surplus
        for i in free:
            more = min(limit - given[i], max(1, budget * portions[i] // mass), surplus)
            given[i] = given[i] + more
            surplus = surplus - more
    return np.array(given)


def noise(own_key, shape, scale, limit, shards=(), kind=jnp.bfloat16):
    entries = scale * jax.random.normal(own_key, shape, jnp.float32)
    if shards:
        entries = entries * block_levels(own_key, shape, shards, -0.22, 0.18)
    return jnp.clip(entries, -limit, limit).astype(kind)


def setup_inputs(seed: int = 0) -> dict:
    seeds = jax.random.split(jax.random.key(seed), 14)
    queries = draw_queries(jax.random.fold_in(seeds[13], 71), 0)
    k_cache = draw_k_cache(jax.random.fold_in(seeds[13], 71), 0)
    v_cache = noise(seeds[2], (ROWS, CTX, KV_HEADS * HEAD_DIM), 1.0, 6.0, ((0, 32), (1, 4)))
    k_new = noise(seeds[3], (ROWS, KV_HEADS * HEAD_DIM), 2.5, 10.0, ((0, 32),))
    v_new = noise(seeds[4], (ROWS, KV_HEADS * HEAD_DIM), 1.0, 6.0, ((0, 32),))
    lengths = draw_lengths(jax.random.fold_in(seeds[13], 71), 0)
    residual = draw_residual(jax.random.fold_in(seeds[13], 71), 0)
    norm_gain = jnp.clip(1.0 + 0.18 * jax.random.normal(seeds[7], (D,), jnp.float32), 0.1, 1.9)
    expert_ids_keys = jax.random.split(jax.random.fold_in(seeds[8], 1), ROWS // ROW_DEV)
    expert_ids_turns = jax.random.permutation(jax.random.fold_in(seeds[8], 3), ROWS // ROW_DEV)
    expert_ids = jax.vmap(lambda own, number: shared_out(jax.random.fold_in(seeds[8], 2), own, number, ROW_DEV, EXPERTS, 2, ROW_DEV, 2))(expert_ids_keys, expert_ids_turns).reshape((ROWS, 2))
    combine_weights = jnp.clip(0.2 + 0.8 * jax.random.uniform(seeds[9], (ROWS, 2), jnp.float32) ** block_levels(seeds[9], (ROWS, 2), ((0, 32),), -0.2, 0.2), 0.2, 1.0)
    w_gate = noise(seeds[10], (EXPERTS, D, FF), D ** -0.5, 0.078125, ((0, 4), (2, 32)))
    w_up = noise(seeds[11], (EXPERTS, D, FF), D ** -0.5, 0.078125, ((0, 4), (2, 32)))
    w_down = noise(seeds[12], (EXPERTS, FF, D), FF ** -0.5, 0.046875, ((0, 4), (1, 32)))
    return dict(queries=queries, k_cache=k_cache, v_cache=v_cache, k_new=k_new, v_new=v_new, lengths=lengths, residual=residual, norm_gain=norm_gain, expert_ids=expert_ids, combine_weights=combine_weights, w_gate=w_gate, w_up=w_up, w_down=w_down)


def reference(queries, k_cache, v_cache, k_new, v_new, lengths, residual, norm_gain, expert_ids, combine_weights, w_gate, w_up, w_down):
    groups = HEADS // KV_HEADS
    factor = HEAD_DIM ** (-0.5)

    def one_row(inputs):
        query_row, key_row, value_row, key_own, value_own, length_row = inputs
        query_heads = query_row.astype(jnp.float32).reshape(KV_HEADS, groups, HEAD_DIM)
        key_heads = key_row.astype(jnp.float32).reshape(CTX, KV_HEADS, HEAD_DIM)
        value_heads = value_row.astype(jnp.float32).reshape(CTX, KV_HEADS, HEAD_DIM)
        scores = jnp.einsum('hgd,chd->hgc', query_heads, key_heads) * factor
        own = jnp.einsum('hgd,hd->hg', query_heads, key_own.astype(jnp.float32).reshape(KV_HEADS, HEAD_DIM)) * factor
        valid = jnp.arange(CTX, dtype=jnp.int32) < length_row
        peak = jnp.maximum(lax.optimization_barrier(jnp.max(jnp.where(valid, scores, -1e+30), axis=-1)), own)
        weights = jnp.where(valid, jnp.exp(scores - peak[..., None]), 0.0)
        fresh = jnp.exp(own - peak)
        denom = lax.optimization_barrier(jnp.sum(weights, axis=-1)) + fresh
        rounded = lax.optimization_barrier(weights.astype(jnp.bfloat16)).astype(jnp.float32)
        numer = jnp.einsum('hgc,chd->hgd', rounded, value_heads)
        numer = numer + fresh[..., None] * value_own.astype(jnp.float32).reshape(KV_HEADS, 1, HEAD_DIM)
        return (numer / denom[..., None]).reshape(D)
    attn = lax.map(one_row, (queries, k_cache, v_cache, k_new, v_new, lengths))
    hidden_state = (residual.astype(jnp.float32) + attn).astype(jnp.bfloat16)
    hidden_f = hidden_state.astype(jnp.float32)
    mean_sq = lax.optimization_barrier(jnp.mean(hidden_f * hidden_f, axis=-1, keepdims=True))
    normed = (hidden_f * lax.rsqrt(mean_sq + 1e-05) * norm_gain).astype(jnp.bfloat16)

    def one_expert(expert_index):
        gate = jnp.dot(normed, w_gate[expert_index], preferred_element_type=jnp.float32)
        upper = jnp.dot(normed, w_up[expert_index], preferred_element_type=jnp.float32)
        act = (jax.nn.silu(gate) * upper).astype(jnp.bfloat16)
        return jnp.dot(act, w_down[expert_index], preferred_element_type=jnp.float32).astype(jnp.bfloat16)
    expert_out = lax.map(one_expert, jnp.arange(EXPERTS, dtype=jnp.int32))
    row_index = jnp.arange(ROWS, dtype=jnp.int32)
    mixture = jnp.zeros((ROWS, D), jnp.float32)
    for choice_index in range(2):
        picked = expert_out[expert_ids[:, choice_index], row_index].astype(jnp.float32)
        mixture = mixture + combine_weights[:, choice_index][:, None] * picked
    layer_out = (hidden_f + mixture).astype(jnp.bfloat16)
    return (hidden_state, layer_out)
```

```python
import jax
import jax.numpy as jnp
from jax import lax
from jax.experimental import pallas as pl
from jax.experimental.pallas import tpu as pltpu
from jax.sharding import Mesh, PartitionSpec as P

HEADS = 48
KV_HEADS = 8
HEAD_DIM = 128
GROUPS = HEADS // KV_HEADS
D = HEADS * HEAD_DIM
SEQ = 4
CTX_HERE = 768
PAY = 112
FF_HERE = 512
BLK = 24
MIB = 1 << 20
NEG = -1e30


def head_masks(shape):
    line = lax.broadcasted_iota(jnp.int32, shape, 0)
    return [(line >= GROUPS * k) & (line < GROUPS * (k + 1)) for k in range(KV_HEADS)]


def spread_heads(row, masks):
    out = jnp.zeros((HEADS, HEAD_DIM), jnp.float32)
    for k in range(KV_HEADS):
        piece = jnp.broadcast_to(row[:, k * HEAD_DIM : (k + 1) * HEAD_DIM], (HEADS, HEAD_DIM))
        out = jnp.where(masks[k], piece, out)
    return out


def attention_kernel(len_ref, q_ref, kn_ref, vn_ref, k_hbm, v_hbm, out_ref, kbuf, vbuf, qs, sems):
    seq = lax.axis_index("seq")
    copies = []
    for r in range(2):
        ck = pltpu.make_async_copy(k_hbm.at[r], kbuf.at[r], sems.at[2 * r])
        cv = pltpu.make_async_copy(v_hbm.at[r], vbuf.at[r], sems.at[2 * r + 1])
        ck.start()
        cv.start()
        copies.append((ck, cv))
    factor = HEAD_DIM ** (-0.5)
    masks = head_masks((HEADS, HEAD_DIM))
    queries = q_ref[...].astype(jnp.float32)
    keys_new = kn_ref[...].astype(jnp.float32)
    values_new = vn_ref[...].astype(jnp.float32)
    line = lax.broadcasted_iota(jnp.int32, (HEADS, HEAD_DIM), 0)
    lane = lax.broadcasted_iota(jnp.int32, (HEADS, HEAD_DIM), 1)
    position = lax.broadcasted_iota(jnp.int32, (HEADS, CTX_HERE), 1) + seq * CTX_HERE
    lse_row = jnp.zeros((1, HEAD_DIM), jnp.float32)
    for r in range(2):
        for h in range(HEADS):
            qs[r * HEADS + h : r * HEADS + h + 1, :] = queries[
                r : r + 1, h * HEAD_DIM : (h + 1) * HEAD_DIM
            ]
        q = qs[r * HEADS : (r + 1) * HEADS, :]
        wide = jnp.concatenate([jnp.where(m, q, 0.0) for m in masks], axis=1).astype(jnp.bfloat16)
        own = jnp.sum(q * spread_heads(keys_new[r : r + 1], masks), axis=1, keepdims=True) * factor
        own = jnp.where(seq == 0, own, NEG)
        copies[r][0].wait()
        scores = (
            lax.dot_general(
                wide, kbuf[r], (((1,), (1,)), ((), ())), preferred_element_type=jnp.float32
            )
            * factor
        )
        valid = position < len_ref[r]
        scores = jnp.where(valid, scores, NEG)
        top = jnp.maximum(jnp.max(scores, axis=1, keepdims=True), own)
        probs = jnp.where(valid, jnp.exp(scores - top), 0.0)
        fresh = jnp.where(seq == 0, jnp.exp(own - top), 0.0)
        total = jnp.sum(probs, axis=1, keepdims=True) + fresh
        copies[r][1].wait()
        pv = jnp.dot(probs.astype(jnp.bfloat16), vbuf[r], preferred_element_type=jnp.float32)
        acc = fresh * spread_heads(values_new[r : r + 1], masks)
        for k in range(KV_HEADS):
            acc = acc + jnp.where(masks[k], pv[:, k * HEAD_DIM : (k + 1) * HEAD_DIM], 0.0)
        some = total > 0.0
        safe = jnp.where(some, total, 1.0)
        lse = jnp.where(some, top + jnp.log(safe), NEG)
        out_ref[r * HEADS : (r + 1) * HEADS, :] = (acc / safe).astype(jnp.bfloat16)
        lse_row = lse_row + jnp.sum(
            jnp.where(lane == line + r * HEADS, lse, 0.0), axis=0, keepdims=True
        )
    hi = lse_row.astype(jnp.bfloat16).astype(jnp.float32)
    mid = (lse_row - hi).astype(jnp.bfloat16).astype(jnp.float32)
    low = lse_row - hi - mid
    tail = lax.broadcasted_iota(jnp.int32, (16, HEAD_DIM), 0)
    tile = jnp.where(tail == 0, hi, jnp.where(tail == 1, mid, jnp.where(tail == 2, low, 0.0)))
    out_ref[2 * HEADS : PAY, :] = tile.astype(jnp.bfloat16)


def combine_kernel(ids_ref, cw_ref, p0, p1, p2, p3, res_ref, pay_ref, hid_ref, rs):
    seq = lax.axis_index("seq")
    residual = res_ref[...].astype(jnp.float32)
    for r in range(2):
        for h in range(HEADS):
            rs[r * HEADS + h : r * HEADS + h + 1, :] = residual[
                r : r + 1, h * HEAD_DIM : (h + 1) * HEAD_DIM
            ]
    line = lax.broadcasted_iota(jnp.int32, (2 * HEADS, HEAD_DIM), 0)
    lane = lax.broadcasted_iota(jnp.int32, (2 * HEADS, HEAD_DIM), 1)
    lses, outs = [], []
    for ref in (p0, p1, p2, p3):
        outs.append(ref[0 : 2 * HEADS, :].astype(jnp.float32))
        side = ref[2 * HEADS : PAY, :].astype(jnp.float32)
        row = side[0:1, :] + side[1:2, :] + side[2:3, :]
        lses.append(jnp.sum(jnp.where(lane == line, row, 0.0), axis=1, keepdims=True))
    top = jnp.maximum(jnp.maximum(lses[0], lses[1]), jnp.maximum(lses[2], lses[3]))
    scales = [jnp.exp(v - top) for v in lses]
    total = (scales[0] + scales[1]) + (scales[2] + scales[3])
    acc = (scales[0] * outs[0] + scales[1] * outs[1]) + (scales[2] * outs[2] + scales[3] * outs[3])
    hidden = (rs[...] + acc / total).astype(jnp.bfloat16)
    rs[...] = hidden.astype(jnp.float32)
    tail = lax.broadcasted_iota(jnp.int32, (16, HEAD_DIM), 0)
    tail_lane = lax.broadcasted_iota(jnp.int32, (16, HEAD_DIM), 1)
    mix = jnp.zeros((16, HEAD_DIM), jnp.float32)
    for r in range(2):
        for t in range(2):
            expert = ids_ref[r, t]
            here = (tail == r) & ((tail_lane == expert) | (tail_lane == expert + 4))
            mix = jnp.where(here, cw_ref[r, t], mix)
    coarse = mix.astype(jnp.bfloat16).astype(jnp.float32)
    side = jnp.where(tail_lane < 4, coarse, mix - coarse).astype(jnp.bfloat16)
    for j in range(16):
        pay_ref[j, 0 : 2 * HEADS, :] = hidden
        pay_ref[j, 2 * HEADS : PAY, :] = side
    rows = []
    for r in range(2):
        first = r * HEADS + seq * (HEADS // SEQ)
        rows.append(
            jnp.concatenate([rs[pl.ds(first + c, 1), :] for c in range(HEADS // SEQ)], axis=1)
        )
    hid_ref[...] = jnp.concatenate(rows, axis=0).astype(jnp.bfloat16)


def expert_kernel(
    xa, xb, gain_ref, wg_hbm, wu_hbm, wd_hbm, own_ref, sib_ref, wg, wu, wd, flat, lhs, mt, sems
):
    expert = lax.axis_index("expert")
    parts = 6
    kc = D // parts
    gates, ups, downs = [], [], []
    for i in range(parts):
        span = pl.ds(i * kc, kc)
        gates.append(pltpu.make_async_copy(wg_hbm.at[0, span], wg.at[span], sems.at[0, i]))
        ups.append(pltpu.make_async_copy(wu_hbm.at[0, span], wu.at[span], sems.at[1, i]))
        downs.append(pltpu.make_async_copy(wd_hbm.at[0, :, span], wd.at[:, span], sems.at[2, i]))
    for i in range(parts):
        gates[i].start()
        ups[i].start()
    for i in range(parts):
        downs[i].start()
    for half, ref in enumerate((xa, xb)):
        for j in range(16):
            first = (half * 32 + j * 2) * HEADS
            flat[first : first + 2 * HEADS, :] = ref[j, 0 : 2 * HEADS, :].astype(jnp.float32)
            mt[half * 32 + 2 * j : half * 32 + 2 * j + 2, :] = ref[
                j, 2 * HEADS : PAY, :
            ].astype(jnp.float32)[0:2]
    squares = jnp.zeros((64, HEAD_DIM), jnp.float32)
    for h in range(HEADS):
        x = flat[pl.ds(h, 64, stride=HEADS), :]
        squares = squares + x * x
        lhs[:, h * HEAD_DIM : (h + 1) * HEAD_DIM] = (x * gain_ref[h : h + 1, :]).astype(jnp.bfloat16)
    scale = lax.rsqrt(jnp.sum(squares, axis=1, keepdims=True) * (1.0 / D) + 1e-05)
    lane = lax.broadcasted_iota(jnp.int32, (64, HEAD_DIM), 1)
    mine = (lane == expert) | (lane == expert + 4)
    weight = jnp.sum(jnp.where(mine, mt[...], 0.0), axis=1, keepdims=True)
    gate = jnp.zeros((64, FF_HERE), jnp.float32)
    upper = jnp.zeros((64, FF_HERE), jnp.float32)
    for i in range(parts):
        x = lhs[:, i * kc : (i + 1) * kc]
        gates[i].wait()
        gate = gate + jnp.dot(x, wg[i * kc : (i + 1) * kc, :], preferred_element_type=jnp.float32)
        ups[i].wait()
        upper = upper + jnp.dot(x, wu[i * kc : (i + 1) * kc, :], preferred_element_type=jnp.float32)
    gate = gate * scale
    upper = upper * scale
    act = (gate / (1.0 + jnp.exp(-gate)) * upper).astype(jnp.bfloat16)
    for i in range(parts):
        downs[i].wait()
        out = (
            jnp.dot(act, wd[:, i * kc : (i + 1) * kc], preferred_element_type=jnp.float32) * weight
        )
        for g in range(kc // HEAD_DIM):
            place = i * (kc // HEAD_DIM) + g
            first = (place // 12) * (16 * BLK) + place % 12
            piece = out[:, g * HEAD_DIM : (g + 1) * HEAD_DIM]
            flat[pl.ds(first, 32, stride=12), :] = piece[0:32]
            flat[pl.ds(64 * BLK + first, 32, stride=12), :] = piece[32:64]
    own_ref[...] = flat[0 : 64 * BLK, :].astype(jnp.bfloat16)
    sib_ref[...] = flat[64 * BLK : 128 * BLK, :].astype(jnp.bfloat16)


def finish_kernel(parts_ref, hid_ref, out_ref):
    total = jnp.zeros((BLK, HEAD_DIM), jnp.float32)
    for j in range(64):
        total = total + parts_ref[j].astype(jnp.float32)
    rows = [
        jnp.concatenate([total[r * 12 + c : r * 12 + c + 1, :] for c in range(12)], axis=1)
        for r in range(2)
    ]
    mixture = jnp.concatenate(rows, axis=0)
    out_ref[...] = (hid_ref[...].astype(jnp.float32) + mixture).astype(jnp.bfloat16)


VMEM = pl.BlockSpec(memory_space=pltpu.VMEM)
SMEM = pl.BlockSpec(memory_space=pltpu.SMEM)
ANY = pl.BlockSpec(memory_space=pl.ANY)


def params(mib):
    return pltpu.CompilerParams(vmem_limit_bytes=mib * MIB)


def body(
    queries,
    k_cache,
    v_cache,
    k_new,
    v_new,
    lengths,
    residual,
    norm_gain,
    expert_ids,
    combine_weights,
    w_gate,
    w_up,
    w_down,
):
    bf16, f32 = jnp.bfloat16, jnp.float32
    partial = pl.pallas_call(
        attention_kernel,
        out_shape=jax.ShapeDtypeStruct((PAY, HEAD_DIM), bf16),
        in_specs=[SMEM, VMEM, VMEM, VMEM, ANY, ANY],
        out_specs=VMEM,
        scratch_shapes=[
            pltpu.VMEM((2, CTX_HERE, KV_HEADS * HEAD_DIM), bf16),
            pltpu.VMEM((2, CTX_HERE, KV_HEADS * HEAD_DIM), bf16),
            pltpu.VMEM((2 * HEADS, HEAD_DIM), f32),
            pltpu.SemaphoreType.DMA((4,)),
        ],
        compiler_params=params(16),
        name="attention",
    )(lengths, queries, k_new, v_new, k_cache, v_cache)
    others = [
        lax.ppermute(partial, "seq", [(i, (i + k) % SEQ) for i in range(SEQ)]) for k in (1, 3, 2)
    ]
    pay, hidden_part = pl.pallas_call(
        combine_kernel,
        out_shape=(
            jax.ShapeDtypeStruct((16, PAY, HEAD_DIM), bf16),
            jax.ShapeDtypeStruct((2, D // SEQ), bf16),
        ),
        in_specs=[SMEM, SMEM] + [VMEM] * 5,
        out_specs=(VMEM, VMEM),
        scratch_shapes=[pltpu.VMEM((2 * HEADS, HEAD_DIM), f32)],
        compiler_params=params(8),
        name="combine",
    )(expert_ids, combine_weights, partial, *others, residual)
    mine = lax.all_to_all(pay, ("z", "expert"), 0, 0, tiled=True)
    theirs = lax.ppermute(mine, "core", [(0, 1), (1, 0)])
    own_out, sib_out = pl.pallas_call(
        expert_kernel,
        out_shape=(
            jax.ShapeDtypeStruct((64 * BLK, HEAD_DIM), bf16),
            jax.ShapeDtypeStruct((64 * BLK, HEAD_DIM), bf16),
        ),
        in_specs=[VMEM, VMEM, VMEM, ANY, ANY, ANY],
        out_specs=(VMEM, VMEM),
        scratch_shapes=[
            pltpu.VMEM((D, FF_HERE), bf16),
            pltpu.VMEM((D, FF_HERE), bf16),
            pltpu.VMEM((FF_HERE, D), bf16),
            pltpu.VMEM((64 * HEADS, HEAD_DIM), f32),
            pltpu.VMEM((64, D), bf16),
            pltpu.VMEM((64, HEAD_DIM), f32),
            pltpu.SemaphoreType.DMA((3, 6)),
        ],
        compiler_params=params(32),
        name="experts",
    )(mine, theirs, norm_gain.reshape(HEADS, HEAD_DIM), w_gate, w_up, w_down)
    from_sib = lax.ppermute(sib_out, "core", [(0, 1), (1, 0)])
    summed = (own_out.astype(f32) + from_sib.astype(f32)).astype(bf16)
    blocks = lax.all_to_all(
        summed.reshape(64, BLK, HEAD_DIM), ("seq", "z", "expert"), 0, 0, tiled=True
    )
    layer_out = pl.pallas_call(
        finish_kernel,
        out_shape=jax.ShapeDtypeStruct((2, D // SEQ), bf16),
        in_specs=[VMEM, VMEM],
        out_specs=VMEM,
        compiler_params=params(8),
        name="finish",
    )(blocks, hidden_part)
    return hidden_part, layer_out


def solution(mesh):
    fine = Mesh(mesh.devices.reshape(4, 4, 2, 4), ("seq", "z", "core", "expert"))
    rows = ("z", "core", "expert")
    in_specs = (
        P(rows, None),
        P(rows, "seq", None),
        P(rows, "seq", None),
        P(rows, None),
        P(rows, None),
        P(rows),
        P(rows, None),
        P(),
        P(rows, None),
        P(rows, None),
        P("expert", None, ("seq", "z", "core")),
        P("expert", None, ("seq", "z", "core")),
        P("expert", ("seq", "z", "core"), None),
    )
    out_specs = (P(rows, "seq"), P(rows, "seq"))
    return jax.shard_map(body, mesh=fine, in_specs=in_specs, out_specs=out_specs, check_vma=False)
```

```python
import jax
import jax.numpy as jnp
from jax import lax
from jax.experimental import pallas as pl
from jax.experimental.pallas import tpu as pltpu
from jax.sharding import Mesh, PartitionSpec as P

HEADS = 48
KV_HEADS = 8
HEAD_DIM = 128
GROUPS = HEADS // KV_HEADS
D = HEADS * HEAD_DIM
SEQ = 4
CTX_HERE = 768
PAY = 112
FF_HERE = 512
BLK = 24
MIB = 1 << 20
NEG = -1e30


def head_masks(shape):
    line = lax.broadcasted_iota(jnp.int32, shape, 0)
    return [(line >= GROUPS * k) & (line < GROUPS * (k + 1)) for k in range(KV_HEADS)]


def spread_heads(row, masks):
    out = jnp.zeros((HEADS, HEAD_DIM), jnp.float32)
    for k in range(KV_HEADS):
        piece = jnp.broadcast_to(row[:, k * HEAD_DIM : (k + 1) * HEAD_DIM], (HEADS, HEAD_DIM))
        out = jnp.where(masks[k], piece, out)
    return out


def attention_kernel(
    len_hbm,
    q_hbm,
    kn_hbm,
    vn_hbm,
    k_hbm,
    v_hbm,
    out_ref,
    len_ref,
    q_ref,
    kn_ref,
    vn_ref,
    kbuf,
    vbuf,
    qs,
    small_sems,
    big_sems,
):
    seq = lax.axis_index("seq")
    sources = ((q_hbm, q_ref), (kn_hbm, kn_ref), (vn_hbm, vn_ref), (len_hbm, len_ref))
    small = [
        pltpu.make_async_copy(src, dst, small_sems.at[i])
        for i, (src, dst) in enumerate(sources)
    ]
    keys = [pltpu.make_async_copy(k_hbm.at[r], kbuf.at[r], big_sems.at[0, r]) for r in range(2)]
    values = [pltpu.make_async_copy(v_hbm.at[r], vbuf.at[r], big_sems.at[1, r]) for r in range(2)]
    small[0].start()
    keys[0].start()
    for copy in small[1:]:
        copy.start()
    keys[1].start()
    factor = HEAD_DIM ** (-0.5)
    masks = head_masks((HEADS, HEAD_DIM))
    line = lax.broadcasted_iota(jnp.int32, (HEADS, HEAD_DIM), 0)
    lane = lax.broadcasted_iota(jnp.int32, (HEADS, HEAD_DIM), 1)
    position = lax.broadcasted_iota(jnp.int32, (HEADS, CTX_HERE), 1) + seq * CTX_HERE
    small[0].wait()
    queries = q_ref[...].astype(jnp.float32)
    for r in range(2):
        for h in range(HEADS):
            qs[r * HEADS + h : r * HEADS + h + 1, :] = queries[
                r : r + 1, h * HEAD_DIM : (h + 1) * HEAD_DIM
            ]
    for copy in small[1:]:
        copy.wait()
    keys_new = kn_ref[...].astype(jnp.float32)
    values_new = vn_ref[...].astype(jnp.float32)
    wides, owns, firsts = [], [], []
    for r in range(2):
        q = qs[r * HEADS : (r + 1) * HEADS, :]
        wides.append(
            jnp.concatenate([jnp.where(m, q, 0.0) for m in masks], axis=1).astype(jnp.bfloat16)
        )
        own = jnp.sum(q * spread_heads(keys_new[r : r + 1], masks), axis=1, keepdims=True) * factor
        owns.append(jnp.where(seq == 0, own, NEG))
        firsts.append(spread_heads(values_new[r : r + 1], masks))
    probs, totals, tops, fresh = [], [], [], []
    for r in range(2):
        keys[r].wait()
        values[r].start()
    for r in range(2):
        scores = (
            lax.dot_general(
                wides[r], kbuf[r], (((1,), (1,)), ((), ())), preferred_element_type=jnp.float32
            )
            * factor
        )
        valid = position < len_ref[r]
        scores = jnp.where(valid, scores, NEG)
        top = jnp.maximum(jnp.max(scores, axis=1, keepdims=True), owns[r])
        weights = jnp.where(valid, jnp.exp(scores - top), 0.0)
        fresh.append(jnp.where(seq == 0, jnp.exp(owns[r] - top), 0.0))
        totals.append(jnp.sum(weights, axis=1, keepdims=True) + fresh[r])
        tops.append(top)
        probs.append(weights.astype(jnp.bfloat16))
    lse_row = jnp.zeros((1, HEAD_DIM), jnp.float32)
    safes = []
    for r in range(2):
        some = totals[r] > 0.0
        safes.append(jnp.where(some, totals[r], 1.0))
        lse = jnp.where(some, tops[r] + jnp.log(safes[r]), NEG)
        lse_row = lse_row + jnp.sum(
            jnp.where(lane == line + r * HEADS, lse, 0.0), axis=0, keepdims=True
        )
    hi = lse_row.astype(jnp.bfloat16).astype(jnp.float32)
    mid = (lse_row - hi).astype(jnp.bfloat16).astype(jnp.float32)
    low = lse_row - hi - mid
    tail = lax.broadcasted_iota(jnp.int32, (16, HEAD_DIM), 0)
    tile = jnp.where(tail == 0, hi, jnp.where(tail == 1, mid, jnp.where(tail == 2, low, 0.0)))
    out_ref[2 * HEADS : PAY, :] = tile.astype(jnp.bfloat16)
    for r in range(2):
        values[r].wait()
        pv = jnp.dot(probs[r], vbuf[r], preferred_element_type=jnp.float32)
        acc = fresh[r] * firsts[r]
        for k in range(KV_HEADS):
            acc = acc + jnp.where(masks[k], pv[:, k * HEAD_DIM : (k + 1) * HEAD_DIM], 0.0)
        out_ref[r * HEADS : (r + 1) * HEADS, :] = (acc / safes[r]).astype(jnp.bfloat16)


def prepare_kernel(after, res_hbm, gain_hbm, lines_ref, gain_ref, res_ref, sems):
    first = pltpu.make_async_copy(res_hbm, res_ref, sems.at[0])
    second = pltpu.make_async_copy(gain_hbm, gain_ref, sems.at[1])
    first.start()
    second.start()
    first.wait()
    residual = res_ref[...].astype(jnp.float32)
    for r in range(2):
        for h in range(HEADS):
            lines_ref[r * HEADS + h : r * HEADS + h + 1, :] = residual[
                r : r + 1, h * HEAD_DIM : (h + 1) * HEAD_DIM
            ]
    second.wait()


def combine_kernel(ids_ref, cw_ref, p0, p1, p2, p3, res_ref, gain_ref, pay_ref, hid_ref, rs):
    seq = lax.axis_index("seq")
    line = lax.broadcasted_iota(jnp.int32, (2 * HEADS, HEAD_DIM), 0)
    lane = lax.broadcasted_iota(jnp.int32, (2 * HEADS, HEAD_DIM), 1)
    lses, outs = [], []
    for ref in (p0, p1, p2, p3):
        outs.append(ref[0 : 2 * HEADS, :].astype(jnp.float32))
        side = ref[2 * HEADS : PAY, :].astype(jnp.float32)
        row = side[0:1, :] + side[1:2, :] + side[2:3, :]
        lses.append(jnp.sum(jnp.where(lane == line, row, 0.0), axis=1, keepdims=True))
    top = jnp.maximum(jnp.maximum(lses[0], lses[1]), jnp.maximum(lses[2], lses[3]))
    scales = [jnp.exp(v - top) for v in lses]
    total = (scales[0] + scales[1]) + (scales[2] + scales[3])
    acc = (scales[0] * outs[0] + scales[1] * outs[1]) + (scales[2] * outs[2] + scales[3] * outs[3])
    hidden = (res_ref[...] + acc / total).astype(jnp.bfloat16).astype(jnp.float32)
    rs[...] = hidden
    normed = []
    for r in range(2):
        x = hidden[r * HEADS : (r + 1) * HEADS, :]
        square = jnp.sum(jnp.sum(x * x, axis=0, keepdims=True), axis=1, keepdims=True)
        normed.append(x * lax.rsqrt(square * (1.0 / D) + 1e-05) * gain_ref[...])
    normed = jnp.concatenate(normed, axis=0).astype(jnp.bfloat16)
    tail = lax.broadcasted_iota(jnp.int32, (16, HEAD_DIM), 0)
    tail_lane = lax.broadcasted_iota(jnp.int32, (16, HEAD_DIM), 1)
    mix = jnp.zeros((16, HEAD_DIM), jnp.float32)
    for r in range(2):
        for t in range(2):
            expert = ids_ref[r, t]
            here = (tail == r) & ((tail_lane == expert) | (tail_lane == expert + 4))
            mix = jnp.where(here, cw_ref[r, t], mix)
    coarse = mix.astype(jnp.bfloat16).astype(jnp.float32)
    side = jnp.where(tail_lane < 4, coarse, mix - coarse).astype(jnp.bfloat16)
    for j in range(16):
        pay_ref[j, 0 : 2 * HEADS, :] = normed
        pay_ref[j, 2 * HEADS : PAY, :] = side
    rows = []
    for r in range(2):
        first = r * HEADS + seq * (HEADS // SEQ)
        rows.append(
            jnp.concatenate([rs[pl.ds(first + c, 1), :] for c in range(HEADS // SEQ)], axis=1)
        )
    hid_ref[...] = jnp.concatenate(rows, axis=0).astype(jnp.bfloat16)


def expert_kernel(xa, xb, wg, wu, wd, own_ref, sib_ref, flat, lhs, mt):
    expert = lax.axis_index("expert")
    parts = 6
    kc = D // parts
    for half, ref in enumerate((xa, xb)):
        for j in range(16):
            row = half * 32 + 2 * j
            flat[row * HEADS : (row + 2) * HEADS, :] = ref[j, 0 : 2 * HEADS, :].astype(jnp.float32)
            mt[row : row + 2, :] = ref[j, 2 * HEADS : PAY, :].astype(jnp.float32)[0:2]
    for h in range(HEADS):
        x = flat[pl.ds(h, 64, stride=HEADS), :]
        lhs[:, h * HEAD_DIM : (h + 1) * HEAD_DIM] = x.astype(jnp.bfloat16)
    lane = lax.broadcasted_iota(jnp.int32, (64, HEAD_DIM), 1)
    mine = (lane == expert) | (lane == expert + 4)
    weight = jnp.sum(jnp.where(mine, mt[...], 0.0), axis=1, keepdims=True)
    gate = jnp.zeros((64, FF_HERE), jnp.float32)
    upper = jnp.zeros((64, FF_HERE), jnp.float32)
    for i in range(parts):
        x = lhs[:, i * kc : (i + 1) * kc]
        gate = gate + jnp.dot(x, wg[0, i * kc : (i + 1) * kc, :], preferred_element_type=jnp.float32)
        upper = upper + jnp.dot(x, wu[0, i * kc : (i + 1) * kc, :], preferred_element_type=jnp.float32)
    act = (gate / (1.0 + jnp.exp(-gate)) * upper).astype(jnp.bfloat16)
    for i in range(parts):
        out = (
            jnp.dot(act, wd[0, :, i * kc : (i + 1) * kc], preferred_element_type=jnp.float32)
            * weight
        )
        for g in range(kc // HEAD_DIM):
            place = i * (kc // HEAD_DIM) + g
            piece = out[:, g * HEAD_DIM : (g + 1) * HEAD_DIM]
            first = (place // 12) * (16 * BLK) + place % 12
            flat[pl.ds(first, 32, stride=12), :] = piece[0:32]
            flat[pl.ds(64 * BLK + first, 32, stride=12), :] = piece[32:64]
    own_ref[...] = flat[0 : 64 * BLK, :].astype(jnp.bfloat16)
    sib_ref[...] = flat[64 * BLK : 128 * BLK, :].astype(jnp.bfloat16)


def finish_kernel(parts_ref, hid_ref, out_ref):
    total = jnp.zeros((BLK, HEAD_DIM), jnp.float32)
    for j in range(64):
        total = total + parts_ref[j].astype(jnp.float32)
    rows = [
        jnp.concatenate([total[r * 12 + c : r * 12 + c + 1, :] for c in range(12)], axis=1)
        for r in range(2)
    ]
    mixture = jnp.concatenate(rows, axis=0)
    out_ref[...] = (hid_ref[...].astype(jnp.float32) + mixture).astype(jnp.bfloat16)


VMEM = pl.BlockSpec(memory_space=pltpu.VMEM)
SMEM = pl.BlockSpec(memory_space=pltpu.SMEM)
HBM = pl.BlockSpec(memory_space=pltpu.HBM)


def params(mib):
    return pltpu.CompilerParams(vmem_limit_bytes=mib * MIB)


def body(
    queries,
    k_cache,
    v_cache,
    k_new,
    v_new,
    lengths,
    residual,
    norm_gain,
    expert_ids,
    combine_weights,
    w_gate,
    w_up,
    w_down,
):
    bf16, f32 = jnp.bfloat16, jnp.float32
    partial = pl.pallas_call(
        attention_kernel,
        out_shape=pltpu.VMEM((PAY, HEAD_DIM), bf16),
        in_specs=[HBM] * 6,
        out_specs=VMEM,
        scratch_shapes=[
            pltpu.SMEM((2,), jnp.int32),
            pltpu.VMEM((2, D), bf16),
            pltpu.VMEM((2, KV_HEADS * HEAD_DIM), bf16),
            pltpu.VMEM((2, KV_HEADS * HEAD_DIM), bf16),
            pltpu.VMEM((2, CTX_HERE, KV_HEADS * HEAD_DIM), bf16),
            pltpu.VMEM((2, CTX_HERE, KV_HEADS * HEAD_DIM), bf16),
            pltpu.VMEM((2 * HEADS, HEAD_DIM), f32),
            pltpu.SemaphoreType.DMA((4,)),
            pltpu.SemaphoreType.DMA((2, 2)),
        ],
        compiler_params=params(58),
        name="attention",
    )(lengths, queries, k_new, v_new, k_cache, v_cache)
    residual_lines, gain_lines = pl.pallas_call(
        prepare_kernel,
        out_shape=(
            pltpu.VMEM((2 * HEADS, HEAD_DIM), f32),
            pltpu.VMEM((HEADS, HEAD_DIM), f32),
        ),
        in_specs=[pl.BlockSpec(memory_space=pl.ANY), HBM, HBM],
        out_specs=(VMEM, VMEM),
        scratch_shapes=[pltpu.VMEM((2, D), bf16), pltpu.SemaphoreType.DMA((2,))],
        compiler_params=params(8),
        name="prepare",
    )(partial, residual, norm_gain.reshape(HEADS, HEAD_DIM))
    others = [
        lax.ppermute(partial, "seq", [(i, (i + k) % SEQ) for i in range(SEQ)]) for k in (1, 3, 2)
    ]
    pay, hidden_part = pl.pallas_call(
        combine_kernel,
        out_shape=(
            jax.ShapeDtypeStruct((16, PAY, HEAD_DIM), bf16),
            jax.ShapeDtypeStruct((2, D // SEQ), bf16),
        ),
        in_specs=[SMEM, SMEM] + [VMEM] * 6,
        out_specs=(VMEM, VMEM),
        scratch_shapes=[pltpu.VMEM((2 * HEADS, HEAD_DIM), f32)],
        compiler_params=params(8),
        cost_estimate=pl.CostEstimate(
            flops=2_000_000_000_000, bytes_accessed=6_000_000_000, transcendentals=0
        ),
        name="combine",
    )(expert_ids, combine_weights, partial, *others, residual_lines, gain_lines)
    mine = lax.all_to_all(pay, ("z", "expert"), 0, 0, tiled=True)
    theirs = lax.ppermute(mine, "core", [(0, 1), (1, 0)])
    own_out, sib_out = pl.pallas_call(
        expert_kernel,
        out_shape=(
            jax.ShapeDtypeStruct((64 * BLK, HEAD_DIM), bf16),
            jax.ShapeDtypeStruct((64 * BLK, HEAD_DIM), bf16),
        ),
        in_specs=[VMEM] * 5,
        out_specs=(VMEM, VMEM),
        scratch_shapes=[
            pltpu.VMEM((64 * HEADS, HEAD_DIM), f32),
            pltpu.VMEM((64, D), bf16),
            pltpu.VMEM((64, HEAD_DIM), f32),
        ],
        compiler_params=params(8),
        name="experts",
    )(mine, theirs, w_gate, w_up, w_down)
    from_sib = lax.ppermute(sib_out, "core", [(0, 1), (1, 0)])
    summed = (own_out.astype(f32) + from_sib.astype(f32)).astype(bf16)
    blocks = lax.all_to_all(
        summed.reshape(64, BLK, HEAD_DIM), ("seq", "z", "expert"), 0, 0, tiled=True
    )
    layer_out = pl.pallas_call(
        finish_kernel,
        out_shape=jax.ShapeDtypeStruct((2, D // SEQ), bf16),
        in_specs=[VMEM, VMEM],
        out_specs=VMEM,
        compiler_params=params(8),
        name="finish",
    )(blocks, hidden_part)
    return hidden_part, layer_out


def solution(mesh):
    fine = Mesh(mesh.devices.reshape(4, 4, 2, 4), ("seq", "z", "core", "expert"))
    rows = ("z", "core", "expert")
    in_specs = (
        P(rows, None),
        P(rows, "seq", None),
        P(rows, "seq", None),
        P(rows, None),
        P(rows, None),
        P(rows),
        P(rows, None),
        P(),
        P(rows, None),
        P(rows, None),
        P("expert", None, ("seq", "z", "core")),
        P("expert", None, ("seq", "z", "core")),
        P("expert", ("seq", "z", "core"), None),
    )
    out_specs = (P(rows, "seq"), P(rows, "seq"))
    return jax.shard_map(body, mesh=fine, in_specs=in_specs, out_specs=out_specs, check_vma=False)
```

```python
import jax
import jax.numpy as jnp
from jax import lax
from jax.experimental import pallas as pl
from jax.experimental.pallas import tpu as pltpu
from jax.sharding import Mesh, PartitionSpec as P

HEADS = 48
KV_HEADS = 8
EXPERTS = 4
HEAD_DIM = 128
GROUPS = HEADS // KV_HEADS
D = HEADS * HEAD_DIM
SEQ = 4
CTX_HERE = 768
PAY = 112
FF_HERE = 512
BLK = 24
MIB = 1 << 20
NEG = -1e30


def head_masks(shape):
    line = lax.broadcasted_iota(jnp.int32, shape, 0)
    return [(line >= GROUPS * k) & (line < GROUPS * (k + 1)) for k in range(KV_HEADS)]


def spread_heads(row, masks):
    out = jnp.zeros((HEADS, HEAD_DIM), jnp.float32)
    for k in range(KV_HEADS):
        piece = jnp.broadcast_to(row[:, k * HEAD_DIM : (k + 1) * HEAD_DIM], (HEADS, HEAD_DIM))
        out = jnp.where(masks[k], piece, out)
    return out


def attention_kernel(
    len_hbm,
    q_hbm,
    kn_hbm,
    vn_hbm,
    k_hbm,
    v_hbm,
    out_ref,
    len_ref,
    q_ref,
    kn_ref,
    vn_ref,
    kbuf,
    vbuf,
    qs,
    small_sems,
    big_sems,
):
    seq = lax.axis_index("seq")
    sources = ((q_hbm, q_ref), (kn_hbm, kn_ref), (vn_hbm, vn_ref), (len_hbm, len_ref))
    small = [
        pltpu.make_async_copy(src, dst, small_sems.at[i])
        for i, (src, dst) in enumerate(sources)
    ]
    keys = [pltpu.make_async_copy(k_hbm.at[r], kbuf.at[r], big_sems.at[0, r]) for r in range(2)]
    values = [pltpu.make_async_copy(v_hbm.at[r], vbuf.at[r], big_sems.at[1, r]) for r in range(2)]
    small[0].start()
    keys[0].start()
    for copy in small[1:]:
        copy.start()
    keys[1].start()
    factor = HEAD_DIM ** (-0.5)
    masks = head_masks((HEADS, HEAD_DIM))
    line = lax.broadcasted_iota(jnp.int32, (HEADS, HEAD_DIM), 0)
    lane = lax.broadcasted_iota(jnp.int32, (HEADS, HEAD_DIM), 1)
    position = lax.broadcasted_iota(jnp.int32, (HEADS, CTX_HERE), 1) + seq * CTX_HERE
    small[0].wait()
    queries = q_ref[...].astype(jnp.float32)
    for r in range(2):
        for h in range(HEADS):
            qs[r * HEADS + h : r * HEADS + h + 1, :] = queries[
                r : r + 1, h * HEAD_DIM : (h + 1) * HEAD_DIM
            ]
    for copy in small[1:]:
        copy.wait()
    keys_new = kn_ref[...].astype(jnp.float32)
    values_new = vn_ref[...].astype(jnp.float32)
    wides, owns, firsts = [], [], []
    for r in range(2):
        q = qs[r * HEADS : (r + 1) * HEADS, :]
        wides.append(
            jnp.concatenate([jnp.where(m, q, 0.0) for m in masks], axis=1).astype(jnp.bfloat16)
        )
        own = jnp.sum(q * spread_heads(keys_new[r : r + 1], masks), axis=1, keepdims=True) * factor
        owns.append(jnp.where(seq == 0, own, NEG))
        firsts.append(spread_heads(values_new[r : r + 1], masks))
    probs, totals, tops, fresh = [], [], [], []
    for r in range(2):
        keys[r].wait()
        values[r].start()
    for r in range(2):
        scores = (
            lax.dot_general(
                wides[r], kbuf[r], (((1,), (1,)), ((), ())), preferred_element_type=jnp.float32
            )
            * factor
        )
        valid = position < len_ref[r]
        scores = jnp.where(valid, scores, NEG)
        top = jnp.maximum(jnp.max(scores, axis=1, keepdims=True), owns[r])
        weights = jnp.where(valid, jnp.exp(scores - top), 0.0)
        fresh.append(jnp.where(seq == 0, jnp.exp(owns[r] - top), 0.0))
        totals.append(jnp.sum(weights, axis=1, keepdims=True) + fresh[r])
        tops.append(top)
        probs.append(weights.astype(jnp.bfloat16))
    lse_row = jnp.zeros((1, HEAD_DIM), jnp.float32)
    safes = []
    for r in range(2):
        some = totals[r] > 0.0
        safes.append(jnp.where(some, totals[r], 1.0))
        lse = jnp.where(some, tops[r] + jnp.log(safes[r]), NEG)
        lse_row = lse_row + jnp.sum(
            jnp.where(lane == line + r * HEADS, lse, 0.0), axis=0, keepdims=True
        )
    hi = lse_row.astype(jnp.bfloat16).astype(jnp.float32)
    mid = (lse_row - hi).astype(jnp.bfloat16).astype(jnp.float32)
    low = lse_row - hi - mid
    tail = lax.broadcasted_iota(jnp.int32, (16, HEAD_DIM), 0)
    tile = jnp.where(tail == 0, hi, jnp.where(tail == 1, mid, jnp.where(tail == 2, low, 0.0)))
    out_ref[2 * HEADS : PAY, :] = tile.astype(jnp.bfloat16)
    for r in range(2):
        values[r].wait()
        pv = jnp.dot(probs[r], vbuf[r], preferred_element_type=jnp.float32)
        acc = fresh[r] * firsts[r]
        for k in range(KV_HEADS):
            acc = acc + jnp.where(masks[k], pv[:, k * HEAD_DIM : (k + 1) * HEAD_DIM], 0.0)
        out_ref[r * HEADS : (r + 1) * HEADS, :] = (acc / safes[r]).astype(jnp.bfloat16)


def prepare_kernel(
    after, res_hbm, gain_hbm, ids_hbm, cw_hbm, lines_ref, gain_ref, mix_ref, res_ref, ids, cw, sems
):
    pairs = ((res_hbm, res_ref), (gain_hbm, gain_ref), (ids_hbm, ids), (cw_hbm, cw))
    copies = [pltpu.make_async_copy(src, dst, sems.at[i]) for i, (src, dst) in enumerate(pairs)]
    for copy in copies:
        copy.start()
    for copy in copies:
        copy.wait()
    residual = res_ref[...].astype(jnp.float32)
    for r in range(2):
        for h in range(HEADS):
            lines_ref[r * HEADS + h : r * HEADS + h + 1, :] = residual[
                r : r + 1, h * HEAD_DIM : (h + 1) * HEAD_DIM
            ]
    line = lax.broadcasted_iota(jnp.int32, (BLK, HEAD_DIM), 0)
    for e in range(EXPERTS):
        weight = []
        for r in range(2):
            total = 0.0
            for t in range(2):
                total = total + jnp.where(ids[r, t] == e, cw[r, t], 0.0)
            weight.append(total)
        mix_ref[e] = jnp.where(line < BLK // 2, weight[0], weight[1])


def combine_kernel(p0, p1, p2, p3, res_ref, gain_ref, pay_ref, hid_ref, rs):
    seq = lax.axis_index("seq")
    line = lax.broadcasted_iota(jnp.int32, (2 * HEADS, HEAD_DIM), 0)
    lane = lax.broadcasted_iota(jnp.int32, (2 * HEADS, HEAD_DIM), 1)
    lses, outs = [], []
    for ref in (p0, p1, p2, p3):
        outs.append(ref[0 : 2 * HEADS, :].astype(jnp.float32))
        side = ref[2 * HEADS : PAY, :].astype(jnp.float32)
        row = side[0:1, :] + side[1:2, :] + side[2:3, :]
        lses.append(jnp.sum(jnp.where(lane == line, row, 0.0), axis=1, keepdims=True))
    top = jnp.maximum(jnp.maximum(lses[0], lses[1]), jnp.maximum(lses[2], lses[3]))
    scales = [jnp.exp(v - top) for v in lses]
    total = (scales[0] + scales[1]) + (scales[2] + scales[3])
    acc = (scales[0] * outs[0] + scales[1] * outs[1]) + (scales[2] * outs[2] + scales[3] * outs[3])
    hidden = (res_ref[...] + acc / total).astype(jnp.bfloat16).astype(jnp.float32)
    rs[...] = hidden
    normed = []
    for r in range(2):
        x = hidden[r * HEADS : (r + 1) * HEADS, :]
        square = jnp.sum(jnp.sum(x * x, axis=0, keepdims=True), axis=1, keepdims=True)
        normed.append(x * lax.rsqrt(square * (1.0 / D) + 1e-05) * gain_ref[...])
    normed = jnp.concatenate(normed, axis=0).astype(jnp.bfloat16)
    for j in range(16):
        pay_ref[j] = normed
    rows = []
    for r in range(2):
        first = r * HEADS + seq * (HEADS // SEQ)
        rows.append(
            jnp.concatenate([rs[pl.ds(first + c, 1), :] for c in range(HEADS // SEQ)], axis=1)
        )
    hid_ref[...] = jnp.concatenate(rows, axis=0).astype(jnp.bfloat16)


def expert_kernel(xa, xb, wg, wu, wd, own_ref, sib_ref, flat, lhs):
    parts = 6
    kc = D // parts
    for half, ref in enumerate((xa, xb)):
        for j in range(16):
            row = half * 32 + 2 * j
            flat[row * HEADS : (row + 2) * HEADS, :] = ref[j].astype(jnp.float32)
    for h in range(HEADS):
        x = flat[pl.ds(h, 64, stride=HEADS), :]
        lhs[:, h * HEAD_DIM : (h + 1) * HEAD_DIM] = x.astype(jnp.bfloat16)
    gate = jnp.zeros((64, FF_HERE), jnp.float32)
    upper = jnp.zeros((64, FF_HERE), jnp.float32)
    for i in range(parts):
        x = lhs[:, i * kc : (i + 1) * kc]
        gate = gate + jnp.dot(x, wg[0, i * kc : (i + 1) * kc, :], preferred_element_type=jnp.float32)
        upper = upper + jnp.dot(x, wu[0, i * kc : (i + 1) * kc, :], preferred_element_type=jnp.float32)
    act = (gate / (1.0 + jnp.exp(-gate)) * upper).astype(jnp.bfloat16)
    for i in range(parts):
        out = jnp.dot(act, wd[0, :, i * kc : (i + 1) * kc], preferred_element_type=jnp.float32)
        for g in range(kc // HEAD_DIM):
            place = i * (kc // HEAD_DIM) + g
            piece = out[:, g * HEAD_DIM : (g + 1) * HEAD_DIM]
            first = (place // 12) * (16 * BLK) + place % 12
            flat[pl.ds(first, 32, stride=12), :] = piece[0:32]
            flat[pl.ds(64 * BLK + first, 32, stride=12), :] = piece[32:64]
    own_ref[...] = flat[0 : 64 * BLK, :].astype(jnp.bfloat16)
    sib_ref[...] = flat[64 * BLK : 128 * BLK, :].astype(jnp.bfloat16)


def finish_kernel(parts_ref, mix_ref, hid_ref, out_ref, hid_out):
    hid_out[...] = hid_ref[...]
    total = jnp.zeros((BLK, HEAD_DIM), jnp.float32)
    for e in range(EXPERTS):
        group = jnp.zeros((BLK, HEAD_DIM), jnp.float32)
        for j in range(64 // EXPERTS):
            group = group + parts_ref[j * EXPERTS + e].astype(jnp.float32)
        total = total + group * mix_ref[e]
    rows = [
        jnp.concatenate([total[r * 12 + c : r * 12 + c + 1, :] for c in range(12)], axis=1)
        for r in range(2)
    ]
    mixture = jnp.concatenate(rows, axis=0)
    out_ref[...] = (hid_ref[...].astype(jnp.float32) + mixture).astype(jnp.bfloat16)


VMEM = pl.BlockSpec(memory_space=pltpu.VMEM)
HBM = pl.BlockSpec(memory_space=pltpu.HBM)


def params(mib):
    return pltpu.CompilerParams(vmem_limit_bytes=mib * MIB)


def body(
    queries,
    k_cache,
    v_cache,
    k_new,
    v_new,
    lengths,
    residual,
    norm_gain,
    expert_ids,
    combine_weights,
    w_gate,
    w_up,
    w_down,
):
    bf16, f32 = jnp.bfloat16, jnp.float32
    partial = pl.pallas_call(
        attention_kernel,
        out_shape=pltpu.VMEM((PAY, HEAD_DIM), bf16),
        in_specs=[HBM] * 6,
        out_specs=VMEM,
        scratch_shapes=[
            pltpu.SMEM((2,), jnp.int32),
            pltpu.VMEM((2, D), bf16),
            pltpu.VMEM((2, KV_HEADS * HEAD_DIM), bf16),
            pltpu.VMEM((2, KV_HEADS * HEAD_DIM), bf16),
            pltpu.VMEM((2, CTX_HERE, KV_HEADS * HEAD_DIM), bf16),
            pltpu.VMEM((2, CTX_HERE, KV_HEADS * HEAD_DIM), bf16),
            pltpu.VMEM((2 * HEADS, HEAD_DIM), f32),
            pltpu.SemaphoreType.DMA((4,)),
            pltpu.SemaphoreType.DMA((2, 2)),
        ],
        compiler_params=params(58),
        name="attention",
    )(lengths, queries, k_new, v_new, k_cache, v_cache)
    residual_lines, gain_lines, mix_lines = pl.pallas_call(
        prepare_kernel,
        out_shape=(
            pltpu.VMEM((2 * HEADS, HEAD_DIM), f32),
            pltpu.VMEM((HEADS, HEAD_DIM), f32),
            pltpu.VMEM((EXPERTS, BLK, HEAD_DIM), f32),
        ),
        in_specs=[pl.BlockSpec(memory_space=pl.ANY)] + [HBM] * 4,
        out_specs=(VMEM, VMEM, VMEM),
        scratch_shapes=[
            pltpu.VMEM((2, D), bf16),
            pltpu.SMEM((2, 2), jnp.int32),
            pltpu.SMEM((2, 2), f32),
            pltpu.SemaphoreType.DMA((4,)),
        ],
        compiler_params=params(8),
        name="prepare",
    )(partial, residual, norm_gain.reshape(HEADS, HEAD_DIM), expert_ids, combine_weights)
    others = [
        lax.ppermute(partial, "seq", [(i, (i + k) % SEQ) for i in range(SEQ)]) for k in (1, 3, 2)
    ]
    pay, hidden_part = pl.pallas_call(
        combine_kernel,
        out_shape=(
            pltpu.VMEM((16, 2 * HEADS, HEAD_DIM), bf16),
            pltpu.VMEM((2, D // SEQ), bf16),
        ),
        in_specs=[VMEM] * 6,
        out_specs=(VMEM, VMEM),
        scratch_shapes=[pltpu.VMEM((2 * HEADS, HEAD_DIM), f32)],
        compiler_params=params(8),
        cost_estimate=pl.CostEstimate(
            flops=2_000_000_000_000, bytes_accessed=6_000_000_000, transcendentals=0
        ),
        name="combine",
    )(partial, *others, residual_lines, gain_lines)
    mine = lax.all_to_all(pay, ("z", "expert"), 0, 0, tiled=True)
    theirs = lax.ppermute(mine, "core", [(0, 1), (1, 0)])
    own_out, sib_out = pl.pallas_call(
        expert_kernel,
        out_shape=(
            jax.ShapeDtypeStruct((64 * BLK, HEAD_DIM), bf16),
            jax.ShapeDtypeStruct((64 * BLK, HEAD_DIM), bf16),
        ),
        in_specs=[VMEM] * 5,
        out_specs=(VMEM, VMEM),
        scratch_shapes=[
            pltpu.VMEM((64 * HEADS, HEAD_DIM), f32),
            pltpu.VMEM((64, D), bf16),
        ],
        compiler_params=params(8),
        name="experts",
    )(mine, theirs, w_gate, w_up, w_down)
    from_sib = lax.ppermute(sib_out, "core", [(0, 1), (1, 0)])
    summed = (own_out.astype(f32) + from_sib.astype(f32)).astype(bf16)
    blocks = lax.all_to_all(
        summed.reshape(64, BLK, HEAD_DIM), ("seq", "z", "expert"), 0, 0, tiled=True
    )
    layer_out, hidden_out = pl.pallas_call(
        finish_kernel,
        out_shape=(jax.ShapeDtypeStruct((2, D // SEQ), bf16),) * 2,
        in_specs=[VMEM] * 3,
        out_specs=(VMEM, VMEM),
        compiler_params=params(8),
        name="finish",
    )(blocks, mix_lines, hidden_part)
    return hidden_out, layer_out


def solution(mesh):
    fine = Mesh(mesh.devices.reshape(4, 4, 2, 4), ("seq", "z", "core", "expert"))
    rows = ("z", "core", "expert")
    in_specs = (
        P(rows, None),
        P(rows, "seq", None),
        P(rows, "seq", None),
        P(rows, None),
        P(rows, None),
        P(rows),
        P(rows, None),
        P(),
        P(rows, None),
        P(rows, None),
        P("expert", None, ("seq", "z", "core")),
        P("expert", None, ("seq", "z", "core")),
        P("expert", ("seq", "z", "core"), None),
    )
    out_specs = (P(rows, "seq"), P(rows, "seq"))
    return jax.shard_map(body, mesh=fine, in_specs=in_specs, out_specs=out_specs, check_vma=False)
```

```python
import jax
import jax.numpy as jnp
from jax import lax
from jax.experimental import pallas as pl
from jax.experimental.pallas import tpu as pltpu
from jax.sharding import Mesh, PartitionSpec as P

HEADS = 48
KV_HEADS = 8
EXPERTS = 4
HEAD_DIM = 128
GROUPS = HEADS // KV_HEADS
D = HEADS * HEAD_DIM
SEQ = 4
CTX_HERE = 768
PAY = 112
FF_HERE = 512
BLK = 24
MIB = 1 << 20
NEG = -1e30


def head_masks(shape):
    line = lax.broadcasted_iota(jnp.int32, shape, 0)
    return [(line >= GROUPS * k) & (line < GROUPS * (k + 1)) for k in range(KV_HEADS)]


def spread_heads(row, masks):
    out = jnp.zeros((HEADS, HEAD_DIM), jnp.float32)
    for k in range(KV_HEADS):
        piece = jnp.broadcast_to(row[:, k * HEAD_DIM : (k + 1) * HEAD_DIM], (HEADS, HEAD_DIM))
        out = jnp.where(masks[k], piece, out)
    return out


def attention_kernel(
    len_hbm,
    q_hbm,
    kn_hbm,
    vn_hbm,
    k_hbm,
    v_hbm,
    out_ref,
    len_ref,
    q_ref,
    kn_ref,
    vn_ref,
    kbuf,
    vbuf,
    qs,
    small_sems,
    big_sems,
):
    seq = lax.axis_index("seq")
    sources = ((q_hbm, q_ref), (kn_hbm, kn_ref), (vn_hbm, vn_ref), (len_hbm, len_ref))
    small = [
        pltpu.make_async_copy(src, dst, small_sems.at[i])
        for i, (src, dst) in enumerate(sources)
    ]
    keys = [pltpu.make_async_copy(k_hbm.at[r], kbuf.at[r], big_sems.at[0, r]) for r in range(2)]
    values = [pltpu.make_async_copy(v_hbm.at[r], vbuf.at[r], big_sems.at[1, r]) for r in range(2)]
    small[0].start()
    keys[0].start()
    for copy in small[1:]:
        copy.start()
    for copy in keys[1:] + values:
        copy.start(priority=1)
    factor = HEAD_DIM ** (-0.5)
    masks = head_masks((HEADS, HEAD_DIM))
    line = lax.broadcasted_iota(jnp.int32, (HEADS, HEAD_DIM), 0)
    lane = lax.broadcasted_iota(jnp.int32, (HEADS, HEAD_DIM), 1)
    position = lax.broadcasted_iota(jnp.int32, (HEADS, CTX_HERE), 1) + seq * CTX_HERE
    small[0].wait()
    queries = q_ref[...].astype(jnp.float32)
    for r in range(2):
        for h in range(HEADS):
            qs[r * HEADS + h : r * HEADS + h + 1, :] = queries[
                r : r + 1, h * HEAD_DIM : (h + 1) * HEAD_DIM
            ]
    for copy in small[1:]:
        copy.wait()
    keys_new = kn_ref[...].astype(jnp.float32)
    values_new = vn_ref[...].astype(jnp.float32)
    wides, owns, firsts = [], [], []
    for r in range(2):
        q = qs[r * HEADS : (r + 1) * HEADS, :]
        wides.append(
            jnp.concatenate([jnp.where(m, q, 0.0) for m in masks], axis=1).astype(jnp.bfloat16)
        )
        own = jnp.sum(q * spread_heads(keys_new[r : r + 1], masks), axis=1, keepdims=True) * factor
        owns.append(jnp.where(seq == 0, own, NEG))
        firsts.append(spread_heads(values_new[r : r + 1], masks))
    scores = []
    for r in range(2):
        keys[r].wait()
        scores.append(
            lax.dot_general(
                wides[r], kbuf[r], (((1,), (1,)), ((), ())), preferred_element_type=jnp.float32
            )
        )
    probs, totals, tops, fresh = [], [], [], []
    for r in range(2):
        valid = position < len_ref[r]
        score = jnp.where(valid, scores[r] * factor, NEG)
        top = jnp.maximum(jnp.max(score, axis=1, keepdims=True), owns[r])
        weights = jnp.where(valid, jnp.exp(score - top), 0.0)
        fresh.append(jnp.where(seq == 0, jnp.exp(owns[r] - top), 0.0))
        totals.append(jnp.sum(weights, axis=1, keepdims=True) + fresh[r])
        tops.append(top)
        probs.append(weights.astype(jnp.bfloat16))
    lse_row = jnp.zeros((1, HEAD_DIM), jnp.float32)
    safes = []
    for r in range(2):
        some = totals[r] > 0.0
        safes.append(jnp.where(some, totals[r], 1.0))
        lse = jnp.where(some, tops[r] + jnp.log(safes[r]), NEG)
        lse_row = lse_row + jnp.sum(
            jnp.where(lane == line + r * HEADS, lse, 0.0), axis=0, keepdims=True
        )
    hi = lse_row.astype(jnp.bfloat16).astype(jnp.float32)
    mid = (lse_row - hi).astype(jnp.bfloat16).astype(jnp.float32)
    low = lse_row - hi - mid
    tail = lax.broadcasted_iota(jnp.int32, (16, HEAD_DIM), 0)
    tile = jnp.where(tail == 0, hi, jnp.where(tail == 1, mid, jnp.where(tail == 2, low, 0.0)))
    out_ref[2 * HEADS : PAY, :] = tile.astype(jnp.bfloat16)
    for copy in values:
        copy.wait()
    for r in range(2):
        pv = jnp.dot(probs[r], vbuf[r], preferred_element_type=jnp.float32)
        acc = fresh[r] * firsts[r]
        for k in range(KV_HEADS):
            acc = acc + jnp.where(masks[k], pv[:, k * HEAD_DIM : (k + 1) * HEAD_DIM], 0.0)
        out_ref[r * HEADS : (r + 1) * HEADS, :] = (acc / safes[r]).astype(jnp.bfloat16)


def prepare_kernel(
    after, res_hbm, gain_hbm, ids_hbm, cw_hbm, lines_ref, gain_ref, mix_ref, res_ref, ids, cw, sems
):
    pairs = ((res_hbm, res_ref), (gain_hbm, gain_ref), (ids_hbm, ids), (cw_hbm, cw))
    copies = [pltpu.make_async_copy(src, dst, sems.at[i]) for i, (src, dst) in enumerate(pairs)]
    for copy in copies:
        copy.start()
    for copy in copies:
        copy.wait()
    residual = res_ref[...].astype(jnp.float32)
    for r in range(2):
        for h in range(HEADS):
            lines_ref[r * HEADS + h : r * HEADS + h + 1, :] = residual[
                r : r + 1, h * HEAD_DIM : (h + 1) * HEAD_DIM
            ]
    line = lax.broadcasted_iota(jnp.int32, (BLK, HEAD_DIM), 0)
    for e in range(EXPERTS):
        weight = []
        for r in range(2):
            total = 0.0
            for t in range(2):
                total = total + jnp.where(ids[r, t] == e, cw[r, t], 0.0)
            weight.append(total)
        mix_ref[e] = jnp.where(line < BLK // 2, weight[0], weight[1])


def combine_kernel(p0, p1, p2, p3, res_ref, gain_ref, pay_ref, hid_ref, rs):
    seq = lax.axis_index("seq")
    line = lax.broadcasted_iota(jnp.int32, (2 * HEADS, HEAD_DIM), 0)
    lane = lax.broadcasted_iota(jnp.int32, (2 * HEADS, HEAD_DIM), 1)
    lses, outs = [], []
    for ref in (p0, p1, p2, p3):
        outs.append(ref[0 : 2 * HEADS, :].astype(jnp.float32))
        side = ref[2 * HEADS : PAY, :].astype(jnp.float32)
        row = side[0:1, :] + side[1:2, :] + side[2:3, :]
        lses.append(jnp.sum(jnp.where(lane == line, row, 0.0), axis=1, keepdims=True))
    top = jnp.maximum(jnp.maximum(lses[0], lses[1]), jnp.maximum(lses[2], lses[3]))
    scales = [jnp.exp(v - top) for v in lses]
    total = (scales[0] + scales[1]) + (scales[2] + scales[3])
    acc = (scales[0] * outs[0] + scales[1] * outs[1]) + (scales[2] * outs[2] + scales[3] * outs[3])
    hidden = (res_ref[...] + acc / total).astype(jnp.bfloat16).astype(jnp.float32)
    rs[...] = hidden
    normed = []
    for r in range(2):
        x = hidden[r * HEADS : (r + 1) * HEADS, :]
        square = jnp.sum(jnp.sum(x * x, axis=0, keepdims=True), axis=1, keepdims=True)
        normed.append(x * lax.rsqrt(square * (1.0 / D) + 1e-05) * gain_ref[...])
    normed = jnp.concatenate(normed, axis=0).astype(jnp.bfloat16)
    for j in range(16):
        pay_ref[j] = normed
    rows = []
    for r in range(2):
        first = r * HEADS + seq * (HEADS // SEQ)
        rows.append(
            jnp.concatenate([rs[pl.ds(first + c, 1), :] for c in range(HEADS // SEQ)], axis=1)
        )
    hid_ref[...] = jnp.concatenate(rows, axis=0).astype(jnp.bfloat16)


def expert_kernel(xa, xb, wg, wu, wd, own_ref, sib_ref, flat, lhs):
    parts = 6
    kc = D // parts
    for half, ref in enumerate((xa, xb)):
        for j in range(16):
            row = half * 32 + 2 * j
            flat[row * HEADS : (row + 2) * HEADS, :] = ref[j].astype(jnp.float32)
    for h in range(HEADS):
        x = flat[pl.ds(h, 64, stride=HEADS), :]
        lhs[:, h * HEAD_DIM : (h + 1) * HEAD_DIM] = x.astype(jnp.bfloat16)
    gate = jnp.zeros((64, FF_HERE), jnp.float32)
    upper = jnp.zeros((64, FF_HERE), jnp.float32)
    for i in range(parts):
        x = lhs[:, i * kc : (i + 1) * kc]
        gate = gate + jnp.dot(x, wg[0, i * kc : (i + 1) * kc, :], preferred_element_type=jnp.float32)
        upper = upper + jnp.dot(x, wu[0, i * kc : (i + 1) * kc, :], preferred_element_type=jnp.float32)
    act = (gate / (1.0 + jnp.exp(-gate)) * upper).astype(jnp.bfloat16)
    for i in range(parts):
        out = jnp.dot(act, wd[0, :, i * kc : (i + 1) * kc], preferred_element_type=jnp.float32)
        for g in range(kc // HEAD_DIM):
            place = i * (kc // HEAD_DIM) + g
            piece = out[:, g * HEAD_DIM : (g + 1) * HEAD_DIM]
            first = (place // 12) * (16 * BLK) + place % 12
            flat[pl.ds(first, 32, stride=12), :] = piece[0:32]
            flat[pl.ds(64 * BLK + first, 32, stride=12), :] = piece[32:64]
    own_ref[...] = flat[0 : 64 * BLK, :].astype(jnp.bfloat16)
    sib_ref[...] = flat[64 * BLK : 128 * BLK, :].astype(jnp.bfloat16)


def finish_kernel(parts_ref, mix_ref, hid_ref, out_ref, hid_out):
    hid_out[...] = hid_ref[...]
    total = jnp.zeros((BLK, HEAD_DIM), jnp.float32)
    for e in range(EXPERTS):
        group = jnp.zeros((BLK, HEAD_DIM), jnp.float32)
        for j in range(64 // EXPERTS):
            group = group + parts_ref[j * EXPERTS + e].astype(jnp.float32)
        total = total + group * mix_ref[e]
    rows = [
        jnp.concatenate([total[r * 12 + c : r * 12 + c + 1, :] for c in range(12)], axis=1)
        for r in range(2)
    ]
    mixture = jnp.concatenate(rows, axis=0)
    out_ref[...] = (hid_ref[...].astype(jnp.float32) + mixture).astype(jnp.bfloat16)


VMEM = pl.BlockSpec(memory_space=pltpu.VMEM)
HBM = pl.BlockSpec(memory_space=pltpu.HBM)


def params(mib):
    return pltpu.CompilerParams(vmem_limit_bytes=mib * MIB)


def body(
    queries,
    k_cache,
    v_cache,
    k_new,
    v_new,
    lengths,
    residual,
    norm_gain,
    expert_ids,
    combine_weights,
    w_gate,
    w_up,
    w_down,
):
    bf16, f32 = jnp.bfloat16, jnp.float32
    partial = pl.pallas_call(
        attention_kernel,
        out_shape=pltpu.VMEM((PAY, HEAD_DIM), bf16),
        in_specs=[HBM] * 6,
        out_specs=VMEM,
        scratch_shapes=[
            pltpu.SMEM((2,), jnp.int32),
            pltpu.VMEM((2, D), bf16),
            pltpu.VMEM((2, KV_HEADS * HEAD_DIM), bf16),
            pltpu.VMEM((2, KV_HEADS * HEAD_DIM), bf16),
            pltpu.VMEM((2, CTX_HERE, KV_HEADS * HEAD_DIM), bf16),
            pltpu.VMEM((2, CTX_HERE, KV_HEADS * HEAD_DIM), bf16),
            pltpu.VMEM((2 * HEADS, HEAD_DIM), f32),
            pltpu.SemaphoreType.DMA((4,)),
            pltpu.SemaphoreType.DMA((2, 2)),
        ],
        compiler_params=params(58),
        name="attention",
    )(lengths, queries, k_new, v_new, k_cache, v_cache)
    residual_lines, gain_lines, mix_lines = pl.pallas_call(
        prepare_kernel,
        out_shape=(
            pltpu.VMEM((2 * HEADS, HEAD_DIM), f32),
            pltpu.VMEM((HEADS, HEAD_DIM), f32),
            pltpu.VMEM((EXPERTS, BLK, HEAD_DIM), f32),
        ),
        in_specs=[pl.BlockSpec(memory_space=pl.ANY)] + [HBM] * 4,
        out_specs=(VMEM, VMEM, VMEM),
        scratch_shapes=[
            pltpu.VMEM((2, D), bf16),
            pltpu.SMEM((2, 2), jnp.int32),
            pltpu.SMEM((2, 2), f32),
            pltpu.SemaphoreType.DMA((4,)),
        ],
        compiler_params=params(8),
        name="prepare",
    )(partial, residual, norm_gain.reshape(HEADS, HEAD_DIM), expert_ids, combine_weights)
    others = [
        lax.ppermute(partial, "seq", [(i, (i + k) % SEQ) for i in range(SEQ)]) for k in (1, 3, 2)
    ]
    pay, hidden_part = pl.pallas_call(
        combine_kernel,
        out_shape=(
            pltpu.VMEM((16, 2 * HEADS, HEAD_DIM), bf16),
            pltpu.VMEM((2, D // SEQ), bf16),
        ),
        in_specs=[VMEM] * 6,
        out_specs=(VMEM, VMEM),
        scratch_shapes=[pltpu.VMEM((2 * HEADS, HEAD_DIM), f32)],
        compiler_params=params(8),
        cost_estimate=pl.CostEstimate(
            flops=2_000_000_000_000, bytes_accessed=6_000_000_000, transcendentals=0
        ),
        name="combine",
    )(partial, *others, residual_lines, gain_lines)
    mine = lax.all_to_all(pay, ("z", "expert"), 0, 0, tiled=True)
    theirs = lax.ppermute(mine, "core", [(0, 1), (1, 0)])
    own_out, sib_out = pl.pallas_call(
        expert_kernel,
        out_shape=(
            jax.ShapeDtypeStruct((64 * BLK, HEAD_DIM), bf16),
            jax.ShapeDtypeStruct((64 * BLK, HEAD_DIM), bf16),
        ),
        in_specs=[VMEM] * 5,
        out_specs=(VMEM, VMEM),
        scratch_shapes=[
            pltpu.VMEM((64 * HEADS, HEAD_DIM), f32),
            pltpu.VMEM((64, D), bf16),
        ],
        compiler_params=params(8),
        name="experts",
    )(mine, theirs, w_gate, w_up, w_down)
    from_sib = lax.ppermute(sib_out, "core", [(0, 1), (1, 0)])
    summed = (own_out.astype(f32) + from_sib.astype(f32)).astype(bf16)
    blocks = lax.all_to_all(
        summed.reshape(64, BLK, HEAD_DIM), ("seq", "z", "expert"), 0, 0, tiled=True
    )
    layer_out, hidden_out = pl.pallas_call(
        finish_kernel,
        out_shape=(jax.ShapeDtypeStruct((2, D // SEQ), bf16),) * 2,
        in_specs=[VMEM] * 3,
        out_specs=(VMEM, VMEM),
        compiler_params=params(8),
        name="finish",
    )(blocks, mix_lines, hidden_part)
    return hidden_out, layer_out


def solution(mesh):
    fine = Mesh(mesh.devices.reshape(4, 4, 2, 4), ("seq", "z", "core", "expert"))
    rows = ("z", "core", "expert")
    in_specs = (
        P(rows, None),
        P(rows, "seq", None),
        P(rows, "seq", None),
        P(rows, None),
        P(rows, None),
        P(rows),
        P(rows, None),
        P(),
        P(rows, None),
        P(rows, None),
        P("expert", None, ("seq", "z", "core")),
        P("expert", None, ("seq", "z", "core")),
        P("expert", ("seq", "z", "core"), None),
    )
    out_specs = (P(rows, "seq"), P(rows, "seq"))
    return jax.shard_map(body, mesh=fine, in_specs=in_specs, out_specs=out_specs, check_vma=False)
```

```python
import functools

import jax
import jax.numpy as jnp
from jax import lax
from jax.experimental import pallas as pl
from jax.experimental.pallas import tpu as pltpu
from jax.sharding import Mesh, PartitionSpec as P

HEADS = 48
KV_HEADS = 8
EXPERTS = 4
HEAD_DIM = 128
GROUPS = HEADS // KV_HEADS
D = HEADS * HEAD_DIM
SEQ = 4
CTX_HERE = 768
PAY = 112
FF_HERE = 512
BLK = 24
MIB = 1 << 20
NEG = -1e30


def head_masks(shape):
    line = lax.broadcasted_iota(jnp.int32, shape, 0)
    return [(line >= GROUPS * k) & (line < GROUPS * (k + 1)) for k in range(KV_HEADS)]


def spread_heads(row, masks):
    out = jnp.zeros((HEADS, HEAD_DIM), jnp.float32)
    for k in range(KV_HEADS):
        piece = jnp.broadcast_to(row[:, k * HEAD_DIM : (k + 1) * HEAD_DIM], (HEADS, HEAD_DIM))
        out = jnp.where(masks[k], piece, out)
    return out


def attention_kernel(
    len_hbm,
    q_hbm,
    kn_hbm,
    vn_hbm,
    k_hbm,
    v_hbm,
    out_ref,
    len_ref,
    q_ref,
    kn_ref,
    vn_ref,
    kbuf,
    vbuf,
    qs,
    small_sems,
    big_sems,
):
    seq = lax.axis_index("seq")
    sources = ((q_hbm, q_ref), (kn_hbm, kn_ref), (vn_hbm, vn_ref), (len_hbm, len_ref))
    small = [
        pltpu.make_async_copy(src, dst, small_sems.at[i])
        for i, (src, dst) in enumerate(sources)
    ]
    keys = [pltpu.make_async_copy(k_hbm.at[r], kbuf.at[r], big_sems.at[0, r]) for r in range(2)]
    values = [pltpu.make_async_copy(v_hbm.at[r], vbuf.at[r], big_sems.at[1, r]) for r in range(2)]
    small[0].start()
    keys[0].start()
    for copy in small[1:]:
        copy.start()
    keys[1].start(priority=1)
    factor = HEAD_DIM ** (-0.5)
    masks = head_masks((HEADS, HEAD_DIM))
    line = lax.broadcasted_iota(jnp.int32, (HEADS, HEAD_DIM), 0)
    lane = lax.broadcasted_iota(jnp.int32, (HEADS, HEAD_DIM), 1)
    position = lax.broadcasted_iota(jnp.int32, (HEADS, CTX_HERE), 1) + seq * CTX_HERE
    small[0].wait()
    queries = q_ref[...].astype(jnp.float32)
    for r in range(2):
        for h in range(HEADS):
            qs[r * HEADS + h : r * HEADS + h + 1, :] = queries[
                r : r + 1, h * HEAD_DIM : (h + 1) * HEAD_DIM
            ]
    for copy in small[1:]:
        copy.wait()
    reached = [len_ref[r] > seq * CTX_HERE for r in range(2)]
    for r in range(2):
        pl.when(reached[r])(functools.partial(values[r].start, priority=1))
    keys_new = kn_ref[...].astype(jnp.float32)
    values_new = vn_ref[...].astype(jnp.float32)
    wides, owns, firsts = [], [], []
    for r in range(2):
        q = qs[r * HEADS : (r + 1) * HEADS, :]
        wides.append(
            jnp.concatenate([jnp.where(m, q, 0.0) for m in masks], axis=1).astype(jnp.bfloat16)
        )
        own = jnp.sum(q * spread_heads(keys_new[r : r + 1], masks), axis=1, keepdims=True) * factor
        owns.append(jnp.where(seq == 0, own, NEG))
        firsts.append(spread_heads(values_new[r : r + 1], masks))
    scores = []
    for r in range(2):
        keys[r].wait()
        scores.append(
            lax.dot_general(
                wides[r], kbuf[r], (((1,), (1,)), ((), ())), preferred_element_type=jnp.float32
            )
        )
    probs, totals, tops, fresh = [], [], [], []
    for r in range(2):
        valid = position < len_ref[r]
        score = jnp.where(valid, scores[r] * factor, NEG)
        top = jnp.maximum(jnp.max(score, axis=1, keepdims=True), owns[r])
        weights = jnp.where(valid, jnp.exp(score - top), 0.0)
        fresh.append(jnp.where(seq == 0, jnp.exp(owns[r] - top), 0.0))
        totals.append(jnp.sum(weights, axis=1, keepdims=True) + fresh[r])
        tops.append(top)
        probs.append(weights.astype(jnp.bfloat16))
    lse_row = jnp.zeros((1, HEAD_DIM), jnp.float32)
    safes = []
    for r in range(2):
        some = totals[r] > 0.0
        safes.append(jnp.where(some, totals[r], 1.0))
        lse = jnp.where(some, tops[r] + jnp.log(safes[r]), NEG)
        lse_row = lse_row + jnp.sum(
            jnp.where(lane == line + r * HEADS, lse, 0.0), axis=0, keepdims=True
        )
    hi = lse_row.astype(jnp.bfloat16).astype(jnp.float32)
    mid = (lse_row - hi).astype(jnp.bfloat16).astype(jnp.float32)
    low = lse_row - hi - mid
    tail = lax.broadcasted_iota(jnp.int32, (16, HEAD_DIM), 0)
    tile = jnp.where(tail == 0, hi, jnp.where(tail == 1, mid, jnp.where(tail == 2, low, 0.0)))
    out_ref[2 * HEADS : PAY, :] = tile.astype(jnp.bfloat16)
    for r in range(2):
        pl.when(reached[r])(values[r].wait)
    for r in range(2):
        pv = jnp.dot(probs[r], vbuf[r], preferred_element_type=jnp.float32)
        pv = jnp.where(reached[r], pv, 0.0)
        acc = fresh[r] * firsts[r]
        for k in range(KV_HEADS):
            acc = acc + jnp.where(masks[k], pv[:, k * HEAD_DIM : (k + 1) * HEAD_DIM], 0.0)
        out_ref[r * HEADS : (r + 1) * HEADS, :] = (acc / safes[r]).astype(jnp.bfloat16)


def prepare_kernel(
    after, res_hbm, gain_hbm, ids_hbm, cw_hbm, lines_ref, gain_ref, mix_ref, res_ref, ids, cw, sems
):
    pairs = ((res_hbm, res_ref), (gain_hbm, gain_ref), (ids_hbm, ids), (cw_hbm, cw))
    copies = [pltpu.make_async_copy(src, dst, sems.at[i]) for i, (src, dst) in enumerate(pairs)]
    for copy in copies:
        copy.start()
    for copy in copies:
        copy.wait()
    residual = res_ref[...].astype(jnp.float32)
    for r in range(2):
        for h in range(HEADS):
            lines_ref[r * HEADS + h : r * HEADS + h + 1, :] = residual[
                r : r + 1, h * HEAD_DIM : (h + 1) * HEAD_DIM
            ]
    line = lax.broadcasted_iota(jnp.int32, (BLK, HEAD_DIM), 0)
    for e in range(EXPERTS):
        weight = []
        for r in range(2):
            total = 0.0
            for t in range(2):
                total = total + jnp.where(ids[r, t] == e, cw[r, t], 0.0)
            weight.append(total)
        mix_ref[e] = jnp.where(line < BLK // 2, weight[0], weight[1])


def combine_kernel(p0, p1, p2, p3, res_ref, gain_ref, pay_ref, hid_ref, rs):
    seq = lax.axis_index("seq")
    line = lax.broadcasted_iota(jnp.int32, (2 * HEADS, HEAD_DIM), 0)
    lane = lax.broadcasted_iota(jnp.int32, (2 * HEADS, HEAD_DIM), 1)
    lses, outs = [], []
    for ref in (p0, p1, p2, p3):
        outs.append(ref[0 : 2 * HEADS, :].astype(jnp.float32))
        side = ref[2 * HEADS : PAY, :].astype(jnp.float32)
        row = side[0:1, :] + side[1:2, :] + side[2:3, :]
        lses.append(jnp.sum(jnp.where(lane == line, row, 0.0), axis=1, keepdims=True))
    top = jnp.maximum(jnp.maximum(lses[0], lses[1]), jnp.maximum(lses[2], lses[3]))
    scales = [jnp.exp(v - top) for v in lses]
    total = (scales[0] + scales[1]) + (scales[2] + scales[3])
    acc = (scales[0] * outs[0] + scales[1] * outs[1]) + (scales[2] * outs[2] + scales[3] * outs[3])
    hidden = (res_ref[...] + acc / total).astype(jnp.bfloat16).astype(jnp.float32)
    rs[...] = hidden
    normed = []
    for r in range(2):
        x = hidden[r * HEADS : (r + 1) * HEADS, :]
        square = jnp.sum(jnp.sum(x * x, axis=0, keepdims=True), axis=1, keepdims=True)
        normed.append(x * lax.rsqrt(square * (1.0 / D) + 1e-05) * gain_ref[...])
    normed = jnp.concatenate(normed, axis=0).astype(jnp.bfloat16)
    for j in range(16):
        pay_ref[j] = normed
    rows = []
    for r in range(2):
        first = r * HEADS + seq * (HEADS // SEQ)
        rows.append(
            jnp.concatenate([rs[pl.ds(first + c, 1), :] for c in range(HEADS // SEQ)], axis=1)
        )
    hid_ref[...] = jnp.concatenate(rows, axis=0).astype(jnp.bfloat16)


def expert_kernel(xa, xb, wg, wu, wd, own_ref, sib_ref, flat, lhs):
    parts = 6
    kc = D // parts
    for half, ref in enumerate((xa, xb)):
        for j in range(16):
            row = half * 32 + 2 * j
            flat[row * HEADS : (row + 2) * HEADS, :] = ref[j].astype(jnp.float32)
    for h in range(HEADS):
        x = flat[pl.ds(h, 64, stride=HEADS), :]
        lhs[:, h * HEAD_DIM : (h + 1) * HEAD_DIM] = x.astype(jnp.bfloat16)
    gate = jnp.zeros((64, FF_HERE), jnp.float32)
    upper = jnp.zeros((64, FF_HERE), jnp.float32)
    for i in range(parts):
        x = lhs[:, i * kc : (i + 1) * kc]
        gate = gate + jnp.dot(x, wg[0, i * kc : (i + 1) * kc, :], preferred_element_type=jnp.float32)
        upper = upper + jnp.dot(x, wu[0, i * kc : (i + 1) * kc, :], preferred_element_type=jnp.float32)
    act = (gate / (1.0 + jnp.exp(-gate)) * upper).astype(jnp.bfloat16)
    for i in range(parts):
        out = jnp.dot(act, wd[0, :, i * kc : (i + 1) * kc], preferred_element_type=jnp.float32)
        for g in range(kc // HEAD_DIM):
            place = i * (kc // HEAD_DIM) + g
            piece = out[:, g * HEAD_DIM : (g + 1) * HEAD_DIM]
            first = (place // 12) * (16 * BLK) + place % 12
            flat[pl.ds(first, 32, stride=12), :] = piece[0:32]
            flat[pl.ds(64 * BLK + first, 32, stride=12), :] = piece[32:64]
    own_ref[...] = flat[0 : 64 * BLK, :].astype(jnp.bfloat16)
    sib_ref[...] = flat[64 * BLK : 128 * BLK, :].astype(jnp.bfloat16)


def finish_kernel(parts_ref, mix_ref, hid_ref, out_ref, hid_out):
    hid_out[...] = hid_ref[...]
    total = jnp.zeros((BLK, HEAD_DIM), jnp.float32)
    for e in range(EXPERTS):
        group = jnp.zeros((BLK, HEAD_DIM), jnp.float32)
        for j in range(64 // EXPERTS):
            group = group + parts_ref[j * EXPERTS + e].astype(jnp.float32)
        total = total + group * mix_ref[e]
    rows = [
        jnp.concatenate([total[r * 12 + c : r * 12 + c + 1, :] for c in range(12)], axis=1)
        for r in range(2)
    ]
    mixture = jnp.concatenate(rows, axis=0)
    out_ref[...] = (hid_ref[...].astype(jnp.float32) + mixture).astype(jnp.bfloat16)


VMEM = pl.BlockSpec(memory_space=pltpu.VMEM)
HBM = pl.BlockSpec(memory_space=pltpu.HBM)


def params(mib):
    return pltpu.CompilerParams(vmem_limit_bytes=mib * MIB)


def body(
    queries,
    k_cache,
    v_cache,
    k_new,
    v_new,
    lengths,
    residual,
    norm_gain,
    expert_ids,
    combine_weights,
    w_gate,
    w_up,
    w_down,
):
    bf16, f32 = jnp.bfloat16, jnp.float32
    partial = pl.pallas_call(
        attention_kernel,
        out_shape=pltpu.VMEM((PAY, HEAD_DIM), bf16),
        in_specs=[HBM] * 6,
        out_specs=VMEM,
        scratch_shapes=[
            pltpu.SMEM((2,), jnp.int32),
            pltpu.VMEM((2, D), bf16),
            pltpu.VMEM((2, KV_HEADS * HEAD_DIM), bf16),
            pltpu.VMEM((2, KV_HEADS * HEAD_DIM), bf16),
            pltpu.VMEM((2, CTX_HERE, KV_HEADS * HEAD_DIM), bf16),
            pltpu.VMEM((2, CTX_HERE, KV_HEADS * HEAD_DIM), bf16),
            pltpu.VMEM((2 * HEADS, HEAD_DIM), f32),
            pltpu.SemaphoreType.DMA((4,)),
            pltpu.SemaphoreType.DMA((2, 2)),
        ],
        compiler_params=params(58),
        name="attention",
    )(lengths, queries, k_new, v_new, k_cache, v_cache)
    residual_lines, gain_lines, mix_lines = pl.pallas_call(
        prepare_kernel,
        out_shape=(
            pltpu.VMEM((2 * HEADS, HEAD_DIM), f32),
            pltpu.VMEM((HEADS, HEAD_DIM), f32),
            pltpu.VMEM((EXPERTS, BLK, HEAD_DIM), f32),
        ),
        in_specs=[pl.BlockSpec(memory_space=pl.ANY)] + [HBM] * 4,
        out_specs=(VMEM, VMEM, VMEM),
        scratch_shapes=[
            pltpu.VMEM((2, D), bf16),
            pltpu.SMEM((2, 2), jnp.int32),
            pltpu.SMEM((2, 2), f32),
            pltpu.SemaphoreType.DMA((4,)),
        ],
        compiler_params=params(8),
        name="prepare",
    )(partial, residual, norm_gain.reshape(HEADS, HEAD_DIM), expert_ids, combine_weights)
    others = [
        lax.ppermute(partial, "seq", [(i, (i + k) % SEQ) for i in range(SEQ)]) for k in (1, 3, 2)
    ]
    pay, hidden_part = pl.pallas_call(
        combine_kernel,
        out_shape=(
            pltpu.VMEM((16, 2 * HEADS, HEAD_DIM), bf16),
            pltpu.VMEM((2, D // SEQ), bf16),
        ),
        in_specs=[VMEM] * 6,
        out_specs=(VMEM, VMEM),
        scratch_shapes=[pltpu.VMEM((2 * HEADS, HEAD_DIM), f32)],
        compiler_params=params(8),
        cost_estimate=pl.CostEstimate(
            flops=2_000_000_000_000, bytes_accessed=6_000_000_000, transcendentals=0
        ),
        name="combine",
    )(partial, *others, residual_lines, gain_lines)
    mine = lax.all_to_all(pay, ("z", "expert"), 0, 0, tiled=True)
    theirs = lax.ppermute(mine, "core", [(0, 1), (1, 0)])
    own_out, sib_out = pl.pallas_call(
        expert_kernel,
        out_shape=(
            jax.ShapeDtypeStruct((64 * BLK, HEAD_DIM), bf16),
            jax.ShapeDtypeStruct((64 * BLK, HEAD_DIM), bf16),
        ),
        in_specs=[VMEM] * 5,
        out_specs=(VMEM, VMEM),
        scratch_shapes=[
            pltpu.VMEM((64 * HEADS, HEAD_DIM), f32),
            pltpu.VMEM((64, D), bf16),
        ],
        compiler_params=params(8),
        name="experts",
    )(mine, theirs, w_gate, w_up, w_down)
    from_sib = lax.ppermute(sib_out, "core", [(0, 1), (1, 0)])
    summed = (own_out.astype(f32) + from_sib.astype(f32)).astype(bf16)
    blocks = lax.all_to_all(
        summed.reshape(64, BLK, HEAD_DIM), ("seq", "z", "expert"), 0, 0, tiled=True
    )
    layer_out, hidden_out = pl.pallas_call(
        finish_kernel,
        out_shape=(jax.ShapeDtypeStruct((2, D // SEQ), bf16),) * 2,
        in_specs=[VMEM] * 3,
        out_specs=(VMEM, VMEM),
        compiler_params=params(8),
        name="finish",
    )(blocks, mix_lines, hidden_part)
    return hidden_out, layer_out


def solution(mesh):
    fine = Mesh(mesh.devices.reshape(4, 4, 2, 4), ("seq", "z", "core", "expert"))
    rows = ("z", "core", "expert")
    in_specs = (
        P(rows, None),
        P(rows, "seq", None),
        P(rows, "seq", None),
        P(rows, None),
        P(rows, None),
        P(rows),
        P(rows, None),
        P(),
        P(rows, None),
        P(rows, None),
        P("expert", None, ("seq", "z", "core")),
        P("expert", None, ("seq", "z", "core")),
        P("expert", ("seq", "z", "core"), None),
    )
    out_specs = (P(rows, "seq"), P(rows, "seq"))
    return jax.shard_map(body, mesh=fine, in_specs=in_specs, out_specs=out_specs, check_vma=False)
```
